32 devices in a mesh: grp: 2 (over x), row: 4 (over y, core), col: 4 (over z).
Axes of the slice: x: 2, y: 2, z: 4, core: 2. Of those that a mesh axis runs over, the one named last changes fastest.
Arguments:
- pair: bfloat16 [128, 64, 128], P(('grp', 'row'), 'col'), parts along dimension 0, may hold values from -6 to 6
- cotangent: bfloat16 [128, 64, 128], P(('grp', 'row'), 'col'), parts along dimension 0, may hold values from -6 to 6
- token_mask: int32 [128], P('grp'), parts along dimension 0, may hold values from 0 to 1, as said below
- proj_weights: bfloat16 [4, 128, 128], replicated, may hold values from -0.5 to 0.5
- out_weights: bfloat16 [2, 128, 128], replicated, may hold values from -0.5 to 0.5
- norm_gains: float32 [2, 128], replicated, may hold values from 0.5 to 1.5
- norm_biases: float32 [2, 128], replicated, may hold values from -3 to 3
Outputs:
- grad_pair: bfloat16 [128, 64, 128], P(('grp', 'row'), 'col'), parts along dimension 0
- grad_pair_t: bfloat16 [128, 64, 128], P(('grp', 'row'), 'col'), parts along dimension 0
- grad_mats: float32 [12, 128, 128], P('grp'), parts along dimension 0
- grad_norms: float32 [8, 128], P('grp'), parts along dimension 0
The draws below stay inside these ranges and needn't reach their ends.
There are 2 independent parts, one for each index of `grp`. The reference program is written for one: setup_inputs(seed, part) draws one part's arguments, and reference() takes and returns one part's arrays. A program takes and returns all parts, laid end to end along the dimension named above; an argument that names none is the same for every part. Nothing has to cross between parts.
Inputs may be any that keep to these rules, and one draw needn't show every extreme that they name: `token_mask`: 1 on a prefix of the tokens and 0 after it; at least half of the tokens and not all are 1.
All inputs are finite; a program needn't handle non-finite values.
Results may differ from the reference program's by a relative error of at most 0.012.
Values may be sent and summed in bfloat16 or wider, within the bound.
A program may use at most 128 MiB of HBM per device.

```python
import jax
import jax.numpy as jnp
from jax import lax

PAIR = 128
HIDDEN_SIZE = 128
TILE_ROWS = 16
TOKENS = 64
TILE_COLS = 16
N_ROW = 4
N_COL = 4


def draw_token_mask(key, part):
    key = jax.random.fold_in(key, 7)
    length = jax.random.randint(key, (), TOKENS // 2, TOKENS)
    return (jnp.arange(TOKENS) < length).astype(jnp.int32)


def level_of(key, dims, shards, low, high):
    gain = 1.0
    for axis_at, parts in shards:
        heights = jax.random.uniform(jax.random.fold_in(jax.random.fold_in(key, 6), axis_at), (parts,), jnp.float32, low / len(shards), high / len(shards))
        gain = gain * jnp.repeat(jnp.exp(heights), dims[axis_at] // parts).reshape((-1,) + (1,) * (len(dims) - 1 - axis_at))
    return gain


def scatter_about(rng, shape, width, reach, pieces=(), dtype=jnp.bfloat16):
    drawn = width * jax.random.normal(rng, shape, jnp.float32)
    if pieces:
        drawn = drawn * level_of(rng, shape, pieces, -0.22, 0.18)
    return jnp.clip(drawn, -reach, reach).astype(dtype)


def setup_inputs(seed: int = 0, part: int = 0) -> dict:
    seeds = jax.random.split(jax.random.key(seed), 8)
    part_splits = jax.random.split(jax.random.fold_in(seeds[7], part), 8)
    pair = scatter_about(part_splits[0], (TOKENS, TOKENS, PAIR), 1.0, 6.0, ((0, 4), (1, 4)))
    cotangent = scatter_about(part_splits[1], (TOKENS, TOKENS, PAIR), 1.0, 6.0, ((0, 4), (1, 4)))
    token_mask = draw_token_mask(jax.random.fold_in(jax.random.fold_in(seeds[7], part), 71), part)
    proj_weights = scatter_about(seeds[3], (4, PAIR, HIDDEN_SIZE), PAIR ** -0.5, 0.5)
    out_weights = scatter_about(seeds[4], (2, PAIR, PAIR), PAIR ** -0.5, 0.5)
    norm_gains = jnp.clip(jax.random.uniform(seeds[5], (2, PAIR), jnp.float32, 0.5, 1.5), 0.5, 1.5)
    norm_biases = scatter_about(seeds[6], (2, PAIR), 0.5, 3.0, (), jnp.float32)
    return dict(pair=pair, cotangent=cotangent, token_mask=token_mask, proj_weights=proj_weights, out_weights=out_weights, norm_gains=norm_gains, norm_biases=norm_biases)


EPS = 1e-05

def plain_norm(source):
    source = source.astype(jnp.float32)
    center = source - lax.optimization_barrier(jnp.mean(source, axis=-1, keepdims=True))
    spread = lax.rsqrt(lax.optimization_barrier(jnp.mean(center * center, axis=-1, keepdims=True)) + EPS)
    return (center * spread, spread)

def matmul(operand, weight):
    extent = operand.shape
    flattened = operand.reshape(-1, extent[-1])
    result = jnp.dot(flattened, weight, preferred_element_type=jnp.float32)
    return result.reshape(extent[:-1] + (weight.shape[-1],))

def column_sum(values):
    return lax.optimization_barrier(jnp.sum(values.reshape(-1, values.shape[-1]), axis=0))

def outer_sum(first, second):
    return jnp.dot(first.reshape(-1, first.shape[-1]).T, second.reshape(-1, second.shape[-1]), preferred_element_type=jnp.float32)

def project(normed, weight, gate_weight, pair_mask):
    linear = matmul(normed, weight)
    opened = jax.nn.sigmoid(matmul(normed, gate_weight))
    return ((opened * linear * pair_mask).astype(jnp.bfloat16), linear, opened)

def project_back(d_proj, normed, linear, opened, pair_mask, weight, gate_weight):
    upstream = d_proj.astype(jnp.float32) * pair_mask
    d_linear = (upstream * opened).astype(jnp.bfloat16)
    d_opened = (upstream * linear * opened * (1.0 - opened)).astype(jnp.bfloat16)
    grad_weight = outer_sum(normed, d_linear)
    grad_gate = outer_sum(normed, d_opened)
    returned = matmul(d_linear, weight.T) + matmul(d_opened, gate_weight.T)
    return (returned, grad_weight, grad_gate)

def norm_back(upstream, normal, spread, gain_vec):
    scaled_up = upstream * gain_vec
    returned = spread * (scaled_up - lax.optimization_barrier(jnp.mean(scaled_up, axis=-1, keepdims=True)) - normal * lax.optimization_barrier(jnp.mean(scaled_up * normal, axis=-1, keepdims=True)))
    return (returned, column_sum(upstream * normal), column_sum(upstream))

def output_back(mixing, normed, cotangent, out_weight, gate_weight, gain_vec, bias_vec):
    normal, spread = plain_norm(mixing)
    ynorm = (normal * gain_vec + bias_vec).astype(jnp.bfloat16)
    outer = matmul(ynorm, out_weight)
    opened = jax.nn.sigmoid(matmul(normed, gate_weight))
    upstream = cotangent.astype(jnp.float32)
    d_out = (upstream * opened).astype(jnp.bfloat16)
    d_opened = (upstream * outer * opened * (1.0 - opened)).astype(jnp.bfloat16)
    grad_out = outer_sum(ynorm, d_out)
    grad_gate = outer_sum(normed, d_opened)
    d_norm = matmul(d_out, out_weight.T)
    d_mixing, grad_gain, grad_bias = norm_back(d_norm, normal, spread, gain_vec)
    return (d_mixing.astype(jnp.bfloat16), matmul(d_opened, gate_weight.T), grad_out, grad_gate, grad_gain, grad_bias)

def reference(pair, cotangent, token_mask, proj_weights, out_weights, norm_gains, norm_biases):
    presence = token_mask.astype(jnp.float32)
    pair_mask = (presence[:, None] * presence[None, :])[:, :, None]
    normal, spread = plain_norm(pair)
    normed = (normal * norm_gains[0] + norm_biases[0]).astype(jnp.bfloat16)
    left_proj, left_lin, left_open = project(normed, proj_weights[0], proj_weights[1], pair_mask)
    right_proj, right_lin, right_open = project(normed, proj_weights[2], proj_weights[3], pair_mask)
    mixing = jnp.einsum('ikh,jkh->ijh', left_proj.astype(jnp.float32), right_proj.astype(jnp.float32))
    d_mixing, d_gate_in, grad_out, grad_gate, grad_gain, grad_bias = output_back(mixing, normed, cotangent, out_weights[0], out_weights[1], norm_gains[1], norm_biases[1])
    d_left = jnp.zeros(left_proj.shape, jnp.float32)
    for block_index in range(N_COL):
        first_row = block_index * TILE_COLS
        portion = jnp.einsum('ijh,jkh->ikh', d_mixing[:, first_row:first_row + TILE_COLS].astype(jnp.float32), right_proj[first_row:first_row + TILE_COLS].astype(jnp.float32))
        d_left = d_left + lax.optimization_barrier(portion.astype(jnp.bfloat16)).astype(jnp.float32)
    d_right = jnp.zeros(right_proj.shape, jnp.float32)
    for block_index in range(N_ROW):
        first_row = block_index * TILE_ROWS
        portion = jnp.einsum('ijh,ikh->jkh', d_mixing[first_row:first_row + TILE_ROWS].astype(jnp.float32), left_proj[first_row:first_row + TILE_ROWS].astype(jnp.float32))
        d_right = d_right + lax.optimization_barrier(portion.astype(jnp.bfloat16)).astype(jnp.float32)
    back_left, grad_lw, grad_lg = project_back(d_left.astype(jnp.bfloat16), normed, left_lin, left_open, pair_mask, proj_weights[0], proj_weights[1])
    back_right, grad_rw, grad_rg = project_back(d_right.astype(jnp.bfloat16), normed, right_lin, right_open, pair_mask, proj_weights[2], proj_weights[3])
    main_back, gain_main, bias_main = norm_back(back_left + d_gate_in, normal, spread, norm_gains[0])
    side_back, gain_side, bias_side = norm_back(back_right, normal, spread, norm_gains[0])
    grad_pair = main_back.astype(jnp.bfloat16)
    grad_pair_t = jnp.transpose(side_back, (1, 0, 2)).astype(jnp.bfloat16)
    grad_mats = jnp.stack([grad_lw, grad_lg, grad_rw, grad_rg, grad_out, grad_gate]) / TOKENS
    grad_norms = jnp.stack([gain_main + gain_side, bias_main + bias_side, grad_gain, grad_bias]) / TOKENS
    return (grad_pair, grad_pair_t, grad_mats, grad_norms)
```

```python
import functools

import jax
import jax.numpy as jnp
from jax import lax
from jax.experimental import pallas as pl
from jax.experimental.pallas import tpu as pltpu
from jax.sharding import PartitionSpec as P

MESH = pl.DeviceIdType.MESH
F32 = jnp.float32
BF16 = jnp.bfloat16

EPS = 1e-05


def spread_2(x, axis, root):
    mine = lax.axis_index(axis) == root
    return lax.psum(jnp.where(mine, x, jnp.zeros_like(x)), axis)


def plain_norm(source):
    source = source.astype(jnp.float32)
    center = source - jnp.mean(source, axis=-1, keepdims=True)
    spread = lax.rsqrt(jnp.mean(center * center, axis=-1, keepdims=True) + EPS)
    return (center * spread, spread)


def matmul(operand, weight):
    extent = operand.shape
    flattened = operand.reshape(-1, extent[-1])
    result = jnp.dot(flattened, weight, preferred_element_type=jnp.float32)
    return result.reshape(extent[:-1] + (weight.shape[-1],))


def column_sum(values):
    return jnp.sum(values.reshape(-1, values.shape[-1]), axis=0)


def outer_sum(first, second):
    return jnp.dot(
        first.reshape(-1, first.shape[-1]).T,
        second.reshape(-1, second.shape[-1]),
        preferred_element_type=jnp.float32,
    )


def project(normed, weight, gate_weight, pair_mask):
    linear = matmul(normed, weight)
    opened = jax.nn.sigmoid(matmul(normed, gate_weight))
    return ((opened * linear * pair_mask).astype(jnp.bfloat16), linear, opened)


def project_back(d_proj, normed, linear, opened, pair_mask, weight, gate_weight):
    upstream = d_proj.astype(jnp.float32) * pair_mask
    d_linear = (upstream * opened).astype(jnp.bfloat16)
    d_opened = (upstream * linear * opened * (1.0 - opened)).astype(jnp.bfloat16)
    grad_weight = outer_sum(normed, d_linear)
    grad_gate = outer_sum(normed, d_opened)
    returned = matmul(d_linear, weight.T) + matmul(d_opened, gate_weight.T)
    return (returned, grad_weight, grad_gate)


def norm_back(upstream, normal, spread, gain_vec):
    scaled_up = upstream * gain_vec
    returned = spread * (
        scaled_up
        - jnp.mean(scaled_up, axis=-1, keepdims=True)
        - normal * jnp.mean(scaled_up * normal, axis=-1, keepdims=True)
    )
    return (returned, column_sum(upstream * normal), column_sum(upstream))


def output_back(mixing, normed, cotangent, out_weight, gate_weight, gain_vec, bias_vec):
    normal, spread = plain_norm(mixing)
    ynorm = (normal * gain_vec + bias_vec).astype(jnp.bfloat16)
    outer = matmul(ynorm, out_weight)
    opened = jax.nn.sigmoid(matmul(normed, gate_weight))
    upstream = cotangent.astype(jnp.float32)
    d_out = (upstream * opened).astype(jnp.bfloat16)
    d_opened = (upstream * outer * opened * (1.0 - opened)).astype(jnp.bfloat16)
    grad_out = outer_sum(ynorm, d_out)
    grad_gate = outer_sum(normed, d_opened)
    d_norm = matmul(d_out, out_weight.T)
    d_mixing, grad_gain, grad_bias = norm_back(d_norm, normal, spread, gain_vec)
    return (
        d_mixing.astype(jnp.bfloat16),
        matmul(d_opened, gate_weight.T),
        grad_out,
        grad_gate,
        grad_gain,
        grad_bias,
    )


def take_cols(values, offset, amount):
    return lax.dynamic_slice_in_dim(values, offset, amount, 1)


def per_device(pair, cotangent, token_mask, proj_weights, out_weights, norm_gains, norm_biases):
    tile_rows = pair.shape[0]
    tile_cols = pair.shape[1]
    tokens = token_mask.shape[0]
    repeat_count = lax.axis_size("row") // lax.axis_size("col")
    row_index = lax.axis_index("row")
    col_index = lax.axis_index("col")
    presence = token_mask.astype(jnp.float32)
    row_presence = lax.dynamic_slice_in_dim(presence, row_index * tile_rows, tile_rows)
    col_presence = lax.dynamic_slice_in_dim(presence, col_index * tile_cols, tile_cols)
    tile_mask = (row_presence[:, None] * col_presence[None, :])[:, :, None]
    gain_in = norm_gains[0]
    bias_in = norm_biases[0]
    strip = lax.all_gather(pair, "col", axis=1, tiled=True)
    strip_normal, strip_spread = plain_norm(strip)
    strip_normed = (strip_normal * gain_in + bias_in).astype(jnp.bfloat16)
    strip_mask = (row_presence[:, None] * presence[None, :])[:, :, None]
    left_rows, strip_lin, strip_open = project(
        strip_normed, proj_weights[0], proj_weights[1], strip_mask
    )
    first_col = col_index * tile_cols
    normal = take_cols(strip_normal, first_col, tile_cols)
    spread = take_cols(strip_spread, first_col, tile_cols)
    normed = take_cols(strip_normed, first_col, tile_cols)
    left_lin = take_cols(strip_lin, first_col, tile_cols)
    left_open = take_cols(strip_open, first_col, tile_cols)
    first_key = row_index * tile_rows
    side_mask = (col_presence[:, None] * row_presence[None, :])[:, :, None]
    pieces = []
    for offset in range(repeat_count):
        pieces.append(spread_2(strip, "row", col_index * repeat_count + offset))
    column_pairs = jnp.concatenate(pieces, axis=0)
    right_normal, right_spread = plain_norm(column_pairs)
    right_normed = (right_normal * gain_in + bias_in).astype(jnp.bfloat16)
    right_mask = (col_presence[:, None] * presence[None, :])[:, :, None]
    right_rows, right_lin, right_open = project(
        right_normed, proj_weights[2], proj_weights[3], right_mask
    )
    side_normal = take_cols(right_normal, first_key, tile_rows)
    side_spread = take_cols(right_spread, first_key, tile_rows)
    side_normed = take_cols(right_normed, first_key, tile_rows)
    side_lin = take_cols(right_lin, first_key, tile_rows)
    side_open = take_cols(right_open, first_key, tile_rows)
    mixing = jnp.einsum("ikh,jkh->ijh", left_rows, right_rows, preferred_element_type=jnp.float32)
    d_mixing, d_gate_in, grad_out, grad_gate, grad_gain, grad_bias = output_back(
        mixing, normed, cotangent, out_weights[0], out_weights[1], norm_gains[1], norm_biases[1]
    )
    portion = take_cols(right_rows, jnp.int32(0), lax.axis_size("col") * tile_cols)
    d_left = lax.psum_scatter(
        jnp.einsum("ijh,jkh->kih", d_mixing, portion, preferred_element_type=jnp.float32).astype(
            jnp.bfloat16
        ),
        "col",
        scatter_dimension=0,
        tiled=True,
    ).astype(jnp.float32)
    d_left = jnp.transpose(d_left, (1, 0, 2)).astype(jnp.bfloat16)
    portion = take_cols(left_rows, jnp.int32(0), lax.axis_size("row") * tile_rows)
    d_right = lax.psum_scatter(
        jnp.einsum("ijh,ikh->kjh", d_mixing, portion, preferred_element_type=jnp.float32).astype(
            jnp.bfloat16
        ),
        "row",
        scatter_dimension=0,
        tiled=True,
    ).astype(jnp.float32)
    d_right = jnp.transpose(d_right, (1, 0, 2)).astype(jnp.bfloat16)
    back_left, grad_lw, grad_lg = project_back(
        d_left, normed, left_lin, left_open, tile_mask, proj_weights[0], proj_weights[1]
    )
    back_right, grad_rw, grad_rg = project_back(
        d_right, side_normed, side_lin, side_open, side_mask, proj_weights[2], proj_weights[3]
    )
    main_back, gain_main, bias_main = norm_back(back_left + d_gate_in, normal, spread, gain_in)
    side_back, gain_side, bias_side = norm_back(back_right, side_normal, side_spread, gain_in)
    matrices = jnp.stack([grad_lw, grad_lg, grad_rw, grad_rg, grad_out, grad_gate])
    vectors = jnp.stack([gain_main + gain_side, bias_main + bias_side, grad_gain, grad_bias])
    matrices, vectors = lax.psum((matrices, vectors), ("row", "col"))
    grad_pair = main_back.astype(jnp.bfloat16)
    grad_pair_t = jnp.transpose(side_back, (1, 0, 2)).astype(jnp.bfloat16)
    return (grad_pair, grad_pair_t, matrices / tokens, vectors / tokens)


def dot_nt(first, second):
    return lax.dot_general(first, second, (((1,), (1,)), ((), ())), preferred_element_type=F32)


def dot_tn(first, second):
    return lax.dot_general(first, second, (((0,), (0,)), ((), ())), preferred_element_type=F32)


def dot_nn(first, second):
    return jnp.dot(first, second, preferred_element_type=F32)


def kernel(
    side,
    tile,
    tokens,
    mask_ref,
    pair_ref,
    cot_ref,
    pw_ref,
    ow_ref,
    gain_ref,
    bias_ref,
    gp_ref,
    gpt_ref,
    gm_ref,
    gn_ref,
    lb,
    rb,
    sr,
    pt,
    lf,
    rf,
    dmix,
    mix,
    normal_s,
    spread_s,
    normed_s,
    lin_s,
    open_s,
    gate_s,
    mask_s,
    tnormal_s,
    tspread_s,
    tnormed_s,
    tlin_s,
    topen_s,
    tmask_s,
    dgate_s,
    tback_s,
    sdl,
    sdr,
    rdl,
    rdr,
    early,
    late,
    rearly,
    rlate,
    aearly,
    alate,
    vec,
    rvec,
    l_send,
    l_recv,
    r_send,
    r_recv,
    p_sem,
    dl_send,
    dl_recv,
    dr_send,
    dr_recv,
    e_send,
    e_recv,
    w_send,
    w_recv,
    ae_send,
    ae_recv,
    aw_send,
    aw_recv,
    v_send,
    v_recv,
):
    r = lax.axis_index("row")
    c = lax.axis_index("col")
    n = side * side
    me = r * side + c
    cells = tile * tile
    erows = early.shape[0] // n
    wrows = late.shape[0] // n

    def at(t):
        return {"row": t // side, "col": lax.rem(t, side)}

    def remote(src, dst, send, recv, row, col):
        return pltpu.make_async_remote_copy(
            src_ref=src,
            dst_ref=dst,
            send_sem=send,
            recv_sem=recv,
            device_id={"row": row, "col": col},
            device_id_type=MESH,
        )

    def others(body):
        def step(p, carry):
            body(lax.rem(me + p, n))
            return carry

        lax.fori_loop(1, n, step, 0)

    barrier = pltpu.get_barrier_semaphore()
    others(
        lambda t: pl.semaphore_signal(barrier, inc=1, device_id=at(t), device_id_type=MESH)
    )

    gain_in = gain_ref[0:1, :]
    bias_in = bias_ref[0:1, :]
    gain_mix = gain_ref[1:2, :]
    bias_mix = bias_ref[1:2, :]

    sub = lax.broadcasted_iota(jnp.int32, (tile, 128), 0)
    row_vec = jnp.zeros((tile, 128), F32)
    col_vec = jnp.zeros((tile, 128), F32)
    row_bits = []
    col_bits = []
    for a in range(tile):
        row_bits.append(mask_ref[r * tile + a].astype(F32))
        col_bits.append(mask_ref[c * tile + a].astype(F32))
        row_vec = jnp.where(sub == a, row_bits[a], row_vec)
        col_vec = jnp.where(sub == a, col_bits[a], col_vec)
    for a in range(tile):
        mask_s[a * tile : (a + 1) * tile, :] = col_vec * row_bits[a]
        tmask_s[a * tile : (a + 1) * tile, :] = row_vec * col_bits[a]

    normal, spread = plain_norm(pair_ref[...].reshape(cells, 128))
    normed = (normal * gain_in + bias_in).astype(BF16)
    normal_s[...] = normal
    spread_s[...] = jnp.broadcast_to(spread, (cells, 128))
    normed_s[...] = normed
    pair_mask = mask_s[...]
    lin = dot_nn(normed, pw_ref[0])
    opened = jax.nn.sigmoid(dot_nn(normed, pw_ref[1]))
    lin_s[...] = lin
    open_s[...] = opened
    lb[c] = (opened * lin * pair_mask).astype(BF16).reshape(tile, tile, 128)
    rlin = dot_nn(normed, pw_ref[2])
    ropen = jax.nn.sigmoid(dot_nn(normed, pw_ref[3]))
    sr[...] = (ropen * rlin * pair_mask).astype(BF16).reshape(tile, tile, 128)

    pl.semaphore_wait(barrier, n - 1)

    def left_copy(d):
        return remote(
            lb.at[c], lb.at[c], l_send.at[d], l_recv.at[c], r, lax.rem(c + d, side)
        )

    def right_copy(d):
        return remote(
            sr, rb.at[c], r_send.at[d], r_recv.at[c], lax.rem(r + d, side), r
        )

    def pair_copy():
        return remote(pair_ref, pt, p_sem.at[0], p_sem.at[1], c, r)

    def left_arrival(b):
        return remote(lb.at[b], lb.at[b], l_send.at[0], l_recv.at[b], r, c)

    def right_arrival(b):
        return remote(sr, rb.at[b], r_send.at[0], r_recv.at[b], r, c)

    for d in range(1, side):
        left_copy(d).start()
        right_copy(d).start()

    @pl.when(r != c)
    def _():
        right_copy(0).start()
        pair_copy().start()

    @pl.when(r == c)
    def _():
        rb[c] = sr[...]
        pt[...] = pair_ref[...]

    gate_s[...] = jax.nn.sigmoid(dot_nn(normed, ow_ref[1]))

    def mix_block(d, accs):
        b = lax.rem(c + d, side)

        @pl.when(d > 0)
        def _():
            left_arrival(b).wait_recv()

        @pl.when(jnp.logical_or(d > 0, r != c))
        def _():
            right_arrival(b).wait_recv()

        base = pl.multiple_of(b * cells, cells)
        lf[pl.ds(base, cells), :] = lb[b].astype(F32).reshape(cells, 128)
        rf[pl.ds(base, cells), :] = rb[b].astype(F32).reshape(cells, 128)

        def step(k, accs):
            right = rf[pl.ds(base + k, tile, stride=tile), :]
            return tuple(
                accs[i] + lf[pl.ds(base + i * tile + k, 1), :] * right for i in range(tile)
            )

        return lax.fori_loop(0, tile, step, accs)

    zero = jnp.zeros((tile, 128), F32)
    accs = lax.fori_loop(0, side, mix_block, (zero,) * tile)
    for i in range(tile):
        mix[i * tile : (i + 1) * tile, :] = accs[i]

    xhat, mspread = plain_norm(mix[...])
    ynorm = (xhat * gain_mix + bias_mix).astype(BF16)
    upstream = cot_ref[...].reshape(cells, 128).astype(F32)
    gate = gate_s[...]
    d_out = (upstream * gate).astype(BF16)
    d_norm = dot_nt(d_out, ow_ref[0])
    scaled = d_norm * gain_mix
    d_mixing = mspread * (
        scaled
        - jnp.mean(scaled, axis=-1, keepdims=True)
        - xhat * jnp.mean(scaled * xhat, axis=-1, keepdims=True)
    )
    dmix[...] = d_mixing.astype(BF16).astype(F32)
    vec[...] = jnp.zeros_like(vec)
    vec[2:3, :] = jnp.sum(d_norm * xhat, axis=0, keepdims=True)
    vec[3:4, :] = jnp.sum(d_norm, axis=0, keepdims=True)
    outer = dot_nn(ynorm, ow_ref[0])
    d_open = (upstream * outer * gate * (1.0 - gate)).astype(BF16)
    early[0:128, :] = dot_tn(ynorm, d_out).astype(BF16)
    early[128:256, :] = dot_tn(normed_s[...], d_open).astype(BF16)
    dgate_s[...] = dot_nt(d_open, ow_ref[1])

    def chunk_copy(src, rows, dst, send, recv, t):
        return remote(
            src.at[pl.ds(pl.multiple_of(t * rows, rows), rows)],
            dst.at[me],
            send.at[t],
            recv.at[me],
            t // side,
            lax.rem(t, side),
        )

    def chunk_arrival(src, rows, dst, send, recv, t):
        return remote(
            src.at[pl.ds(0, rows)], dst.at[t], send.at[t], recv.at[t], r, c
        )

    others(lambda t: chunk_copy(early, erows, rearly, e_send, e_recv, t).start())
    rearly[me] = early[pl.ds(pl.multiple_of(me * erows, erows), erows), :]

    group = 4

    def left_part(b, out, slot):
        def step(g, carry):
            first = g * group
            sums = [zero] * group
            for j in range(tile):
                right = rf[pl.ds(pl.multiple_of(b * cells + j * tile, tile), tile), :]
                for q in range(group):
                    sums[q] = sums[q] + dmix[pl.ds((first + q) * tile + j, 1), :] * right
            for q in range(group):
                out[slot, first + q] = sums[q].astype(BF16)
            return carry

        lax.fori_loop(0, tile // group, step, 0)

    def right_part(b, out, slot):
        def step(g, carry):
            first = g * group
            sums = [zero] * group
            for i in range(tile):
                left = lf[pl.ds(pl.multiple_of(b * cells + i * tile, tile), tile), :]
                for q in range(group):
                    sums[q] = sums[q] + dmix[pl.ds(i * tile + first + q, 1), :] * left
            for q in range(group):
                out[slot, first + q] = sums[q].astype(BF16)
            return carry

        lax.fori_loop(0, tile // group, step, 0)

    def dl_copy(b):
        return remote(sdl.at[b], rdl.at[c], dl_send.at[b], dl_recv.at[c], r, b)

    def dr_copy(b):
        return remote(sdr.at[b], rdr.at[r], dr_send.at[b], dr_recv.at[r], b, c)

    def dl_arrival(b):
        return remote(sdl.at[b], rdl.at[b], dl_send.at[b], dl_recv.at[b], r, c)

    def dr_arrival(b):
        return remote(sdr.at[b], rdr.at[b], dr_send.at[b], dr_recv.at[b], r, c)

    def part_step(d, carry):
        b = lax.rem(c + d, side)
        left_part(b, sdl, b)
        dl_copy(b).start()
        b = lax.rem(r + d, side)
        right_part(b, sdr, b)
        dr_copy(b).start()
        return carry

    lax.fori_loop(1, side, part_step, 0)
    left_part(c, rdl, c)
    right_part(r, rdr, r)

    @pl.when(r != c)
    def _():
        pair_copy().wait_recv()

    tnormal, tspread = plain_norm(pt[...].reshape(cells, 128))
    tnormed = (tnormal * gain_in + bias_in).astype(BF16)
    tnormal_s[...] = tnormal
    tspread_s[...] = jnp.broadcast_to(tspread, (cells, 128))
    tnormed_s[...] = tnormed
    tlin_s[...] = dot_nn(tnormed, pw_ref[2])
    topen_s[...] = jax.nn.sigmoid(dot_nn(tnormed, pw_ref[3]))

    others(lambda t: chunk_arrival(early, erows, rearly, e_send, e_recv, t).wait_recv())
    total = rearly[0].astype(F32)
    for s in range(1, n):
        total = total + rearly[s].astype(F32)
    aearly[me] = (total / tokens).astype(BF16)

    def all_copy(buf, send, recv, t):
        return remote(
            buf.at[me], buf.at[me], send.at[t], recv.at[me], t // side, lax.rem(t, side)
        )

    def all_arrival(buf, send, recv, t):
        return remote(buf.at[t], buf.at[t], send.at[t], recv.at[t], r, c)

    others(lambda t: all_copy(aearly, ae_send, ae_recv, t).start())

    def branch_back(received, mask, opened, linear, normed, first):
        total = received[0].astype(F32)
        for s in range(1, side):
            total = total + received[s].astype(F32)
        up = total.astype(BF16).astype(F32).reshape(cells, 128) * mask
        d_lin = (up * opened).astype(BF16)
        d_gate = (up * linear * opened * (1.0 - opened)).astype(BF16)
        late[first * 128 : (first + 1) * 128, :] = dot_tn(normed, d_lin).astype(BF16)
        late[(first + 1) * 128 : (first + 2) * 128, :] = dot_tn(normed, d_gate).astype(BF16)
        return dot_nt(d_lin, pw_ref[first]) + dot_nt(d_gate, pw_ref[first + 1])

    for d in range(1, side):
        dl_arrival(lax.rem(c + d, side)).wait_recv()
    back_left = branch_back(rdl, mask_s[...], open_s[...], lin_s[...], normed_s[...], 0)
    for d in range(1, side):
        dr_arrival(lax.rem(r + d, side)).wait_recv()
    back_right = branch_back(rdr, tmask_s[...], topen_s[...], tlin_s[...], tnormed_s[...], 2)

    others(lambda t: chunk_copy(late, wrows, rlate, w_send, w_recv, t).start())
    rlate[me] = late[pl.ds(pl.multiple_of(me * wrows, wrows), wrows), :]

    main, gain_main, bias_main = norm_back(
        back_left + dgate_s[...], normal_s[...], spread_s[...], gain_in
    )
    turned, gain_side, bias_side = norm_back(
        back_right, tnormal_s[...], tspread_s[...], gain_in
    )
    vec[0:1, :] = (gain_main + gain_side)[None, :]
    vec[1:2, :] = (bias_main + bias_side)[None, :]

    def vec_copy(t):
        return remote(
            vec, rvec.at[me], v_send.at[t], v_recv.at[me], t // side, lax.rem(t, side)
        )

    def vec_arrival(t):
        return remote(vec, rvec.at[t], v_send.at[t], v_recv.at[t], r, c)

    others(lambda t: vec_copy(t).start())
    rvec[me] = vec[...]
    gp_ref[...] = main.astype(BF16).reshape(tile, tile, 128)
    tback_s[...] = turned
    for k in range(tile):
        gpt_ref[k] = tback_s[pl.ds(k, tile, stride=tile), :].astype(BF16)

    others(lambda t: chunk_arrival(late, wrows, rlate, w_send, w_recv, t).wait_recv())
    total = rlate[0].astype(F32)
    for s in range(1, n):
        total = total + rlate[s].astype(F32)
    alate[me] = (total / tokens).astype(BF16)
    others(lambda t: all_copy(alate, aw_send, aw_recv, t).start())

    others(lambda t: vec_arrival(t).wait_recv())
    total = rvec[0]
    for s in range(1, n):
        total = total + rvec[s]
    gn_ref[...] = total[0:4, :] / tokens

    others(lambda t: all_arrival(aearly, ae_send, ae_recv, t).wait_recv())
    gm_ref[4:6] = aearly[...].astype(F32).reshape(2, 128, 128)

    for d in range(1, side):
        left_copy(d).wait_send()
        right_copy(d).wait_send()
        dl_copy(lax.rem(c + d, side)).wait_send()
        dr_copy(lax.rem(r + d, side)).wait_send()

    @pl.when(r != c)
    def _():
        right_copy(0).wait_send()
        pair_copy().wait_send()

    def sent(t):
        chunk_copy(early, erows, rearly, e_send, e_recv, t).wait_send()
        chunk_copy(late, wrows, rlate, w_send, w_recv, t).wait_send()
        all_copy(aearly, ae_send, ae_recv, t).wait_send()
        vec_copy(t).wait_send()

    others(sent)
    others(lambda t: all_arrival(alate, aw_send, aw_recv, t).wait_recv())
    gm_ref[0:4] = alate[...].astype(F32).reshape(4, 128, 128)
    others(lambda t: all_copy(alate, aw_send, aw_recv, t).wait_send())


def fused(side, pair, cotangent, token_mask, proj_weights, out_weights, norm_gains, norm_biases):
    tile = pair.shape[0]
    tokens = token_mask.shape[0]
    n = side * side
    cells = tile * tile
    erows = 256 // n
    wrows = 512 // n
    block = (side, tile, tile, 128)
    wide = pltpu.VMEM((cells, 128), F32)
    slim = pltpu.VMEM((cells, 128), BF16)
    dma = pltpu.SemaphoreType.DMA
    vmem = pl.BlockSpec(memory_space=pltpu.VMEM)
    return pl.pallas_call(
        functools.partial(kernel, side, tile, tokens),
        out_shape=(
            jax.ShapeDtypeStruct((tile, tile, 128), BF16),
            jax.ShapeDtypeStruct((tile, tile, 128), BF16),
            jax.ShapeDtypeStruct((6, 128, 128), F32),
            jax.ShapeDtypeStruct((4, 128), F32),
        ),
        in_specs=[pl.BlockSpec(memory_space=pltpu.SMEM)] + [vmem] * 6,
        out_specs=(vmem,) * 4,
        scratch_shapes=[
            pltpu.VMEM(block, BF16),
            pltpu.VMEM(block, BF16),
            pltpu.VMEM((tile, tile, 128), BF16),
            pltpu.VMEM((tile, tile, 128), BF16),
            pltpu.VMEM((side * cells, 128), F32),
            pltpu.VMEM((side * cells, 128), F32),
            wide,
            wide,
            wide,
            wide,
            slim,
            wide,
            wide,
            wide,
            wide,
            wide,
            wide,
            slim,
            wide,
            wide,
            wide,
            wide,
            wide,
            pltpu.VMEM(block, BF16),
            pltpu.VMEM(block, BF16),
            pltpu.VMEM(block, BF16),
            pltpu.VMEM(block, BF16),
            pltpu.VMEM((256, 128), BF16),
            pltpu.VMEM((512, 128), BF16),
            pltpu.VMEM((n, erows, 128), BF16),
            pltpu.VMEM((n, wrows, 128), BF16),
            pltpu.VMEM((n, erows, 128), BF16),
            pltpu.VMEM((n, wrows, 128), BF16),
            pltpu.VMEM((8, 128), F32),
            pltpu.VMEM((n, 8, 128), F32),
            dma((side,)),
            dma((side,)),
            dma((side,)),
            dma((side,)),
            dma((2,)),
            dma((side,)),
            dma((side,)),
            dma((side,)),
            dma((side,)),
        ]
        + [dma((n,))] * 10,
        compiler_params=pltpu.CompilerParams(
            collective_id=0, has_side_effects=True, vmem_limit_bytes=40 * 1024 * 1024
        ),
    )(token_mask, pair, cotangent, proj_weights, out_weights, norm_gains, norm_biases)


def device_program(*args):
    rows, cols = lax.axis_size("row"), lax.axis_size("col")
    pair = args[0]
    square = rows == cols and pair.shape[0] == pair.shape[1] == 16
    if square and 256 % (16 * rows * cols) == 0 and pair.shape[2] == 128:
        return fused(rows, *args)
    return per_device(*args)


def solution(mesh):
    in_specs = (
        P(("grp", "row"), "col", None),
        P(("grp", "row"), "col", None),
        P("grp"),
        P(),
        P(),
        P(),
        P(),
    )
    out_specs = (
        P(("grp", "row"), "col", None),
        P(("grp", "row"), "col", None),
        P("grp", None, None),
        P("grp", None),
    )
    return jax.shard_map(
        device_program, mesh=mesh, in_specs=in_specs, out_specs=out_specs, check_vma=False
    )
```

```python
import functools

import jax
import jax.numpy as jnp
from jax import lax
from jax.experimental import pallas as pl
from jax.experimental.pallas import tpu as pltpu
from jax.sharding import PartitionSpec as P

MESH = pl.DeviceIdType.MESH
F32 = jnp.float32
BF16 = jnp.bfloat16

EPS = 1e-05


def spread_2(x, axis, root):
    mine = lax.axis_index(axis) == root
    return lax.psum(jnp.where(mine, x, jnp.zeros_like(x)), axis)


def plain_norm(source):
    source = source.astype(jnp.float32)
    center = source - jnp.mean(source, axis=-1, keepdims=True)
    spread = lax.rsqrt(jnp.mean(center * center, axis=-1, keepdims=True) + EPS)
    return (center * spread, spread)


def matmul(operand, weight):
    extent = operand.shape
    flattened = operand.reshape(-1, extent[-1])
    result = jnp.dot(flattened, weight, preferred_element_type=jnp.float32)
    return result.reshape(extent[:-1] + (weight.shape[-1],))


def column_sum(values):
    return jnp.sum(values.reshape(-1, values.shape[-1]), axis=0)


def outer_sum(first, second):
    return jnp.dot(
        first.reshape(-1, first.shape[-1]).T,
        second.reshape(-1, second.shape[-1]),
        preferred_element_type=jnp.float32,
    )


def project(normed, weight, gate_weight, pair_mask):
    linear = matmul(normed, weight)
    opened = jax.nn.sigmoid(matmul(normed, gate_weight))
    return ((opened * linear * pair_mask).astype(jnp.bfloat16), linear, opened)


def project_back(d_proj, normed, linear, opened, pair_mask, weight, gate_weight):
    upstream = d_proj.astype(jnp.float32) * pair_mask
    d_linear = (upstream * opened).astype(jnp.bfloat16)
    d_opened = (upstream * linear * opened * (1.0 - opened)).astype(jnp.bfloat16)
    grad_weight = outer_sum(normed, d_linear)
    grad_gate = outer_sum(normed, d_opened)
    returned = matmul(d_linear, weight.T) + matmul(d_opened, gate_weight.T)
    return (returned, grad_weight, grad_gate)


def norm_back(upstream, normal, spread, gain_vec):
    scaled_up = upstream * gain_vec
    returned = spread * (
        scaled_up
        - jnp.mean(scaled_up, axis=-1, keepdims=True)
        - normal * jnp.mean(scaled_up * normal, axis=-1, keepdims=True)
    )
    return (returned, column_sum(upstream * normal), column_sum(upstream))


def output_back(mixing, normed, cotangent, out_weight, gate_weight, gain_vec, bias_vec):
    normal, spread = plain_norm(mixing)
    ynorm = (normal * gain_vec + bias_vec).astype(jnp.bfloat16)
    outer = matmul(ynorm, out_weight)
    opened = jax.nn.sigmoid(matmul(normed, gate_weight))
    upstream = cotangent.astype(jnp.float32)
    d_out = (upstream * opened).astype(jnp.bfloat16)
    d_opened = (upstream * outer * opened * (1.0 - opened)).astype(jnp.bfloat16)
    grad_out = outer_sum(ynorm, d_out)
    grad_gate = outer_sum(normed, d_opened)
    d_norm = matmul(d_out, out_weight.T)
    d_mixing, grad_gain, grad_bias = norm_back(d_norm, normal, spread, gain_vec)
    return (
        d_mixing.astype(jnp.bfloat16),
        matmul(d_opened, gate_weight.T),
        grad_out,
        grad_gate,
        grad_gain,
        grad_bias,
    )


def take_cols(values, offset, amount):
    return lax.dynamic_slice_in_dim(values, offset, amount, 1)


def per_device(pair, cotangent, token_mask, proj_weights, out_weights, norm_gains, norm_biases):
    tile_rows = pair.shape[0]
    tile_cols = pair.shape[1]
    tokens = token_mask.shape[0]
    repeat_count = lax.axis_size("row") // lax.axis_size("col")
    row_index = lax.axis_index("row")
    col_index = lax.axis_index("col")
    presence = token_mask.astype(jnp.float32)
    row_presence = lax.dynamic_slice_in_dim(presence, row_index * tile_rows, tile_rows)
    col_presence = lax.dynamic_slice_in_dim(presence, col_index * tile_cols, tile_cols)
    tile_mask = (row_presence[:, None] * col_presence[None, :])[:, :, None]
    gain_in = norm_gains[0]
    bias_in = norm_biases[0]
    strip = lax.all_gather(pair, "col", axis=1, tiled=True)
    strip_normal, strip_spread = plain_norm(strip)
    strip_normed = (strip_normal * gain_in + bias_in).astype(jnp.bfloat16)
    strip_mask = (row_presence[:, None] * presence[None, :])[:, :, None]
    left_rows, strip_lin, strip_open = project(
        strip_normed, proj_weights[0], proj_weights[1], strip_mask
    )
    first_col = col_index * tile_cols
    normal = take_cols(strip_normal, first_col, tile_cols)
    spread = take_cols(strip_spread, first_col, tile_cols)
    normed = take_cols(strip_normed, first_col, tile_cols)
    left_lin = take_cols(strip_lin, first_col, tile_cols)
    left_open = take_cols(strip_open, first_col, tile_cols)
    first_key = row_index * tile_rows
    side_mask = (col_presence[:, None] * row_presence[None, :])[:, :, None]
    pieces = []
    for offset in range(repeat_count):
        pieces.append(spread_2(strip, "row", col_index * repeat_count + offset))
    column_pairs = jnp.concatenate(pieces, axis=0)
    right_normal, right_spread = plain_norm(column_pairs)
    right_normed = (right_normal * gain_in + bias_in).astype(jnp.bfloat16)
    right_mask = (col_presence[:, None] * presence[None, :])[:, :, None]
    right_rows, right_lin, right_open = project(
        right_normed, proj_weights[2], proj_weights[3], right_mask
    )
    side_normal = take_cols(right_normal, first_key, tile_rows)
    side_spread = take_cols(right_spread, first_key, tile_rows)
    side_normed = take_cols(right_normed, first_key, tile_rows)
    side_lin = take_cols(right_lin, first_key, tile_rows)
    side_open = take_cols(right_open, first_key, tile_rows)
    mixing = jnp.einsum("ikh,jkh->ijh", left_rows, right_rows, preferred_element_type=jnp.float32)
    d_mixing, d_gate_in, grad_out, grad_gate, grad_gain, grad_bias = output_back(
        mixing, normed, cotangent, out_weights[0], out_weights[1], norm_gains[1], norm_biases[1]
    )
    portion = take_cols(right_rows, jnp.int32(0), lax.axis_size("col") * tile_cols)
    d_left = lax.psum_scatter(
        jnp.einsum("ijh,jkh->kih", d_mixing, portion, preferred_element_type=jnp.float32).astype(
            jnp.bfloat16
        ),
        "col",
        scatter_dimension=0,
        tiled=True,
    ).astype(jnp.float32)
    d_left = jnp.transpose(d_left, (1, 0, 2)).astype(jnp.bfloat16)
    portion = take_cols(left_rows, jnp.int32(0), lax.axis_size("row") * tile_rows)
    d_right = lax.psum_scatter(
        jnp.einsum("ijh,ikh->kjh", d_mixing, portion, preferred_element_type=jnp.float32).astype(
            jnp.bfloat16
        ),
        "row",
        scatter_dimension=0,
        tiled=True,
    ).astype(jnp.float32)
    d_right = jnp.transpose(d_right, (1, 0, 2)).astype(jnp.bfloat16)
    back_left, grad_lw, grad_lg = project_back(
        d_left, normed, left_lin, left_open, tile_mask, proj_weights[0], proj_weights[1]
    )
    back_right, grad_rw, grad_rg = project_back(
        d_right, side_normed, side_lin, side_open, side_mask, proj_weights[2], proj_weights[3]
    )
    main_back, gain_main, bias_main = norm_back(back_left + d_gate_in, normal, spread, gain_in)
    side_back, gain_side, bias_side = norm_back(back_right, side_normal, side_spread, gain_in)
    matrices = jnp.stack([grad_lw, grad_lg, grad_rw, grad_rg, grad_out, grad_gate])
    vectors = jnp.stack([gain_main + gain_side, bias_main + bias_side, grad_gain, grad_bias])
    matrices, vectors = lax.psum((matrices, vectors), ("row", "col"))
    grad_pair = main_back.astype(jnp.bfloat16)
    grad_pair_t = jnp.transpose(side_back, (1, 0, 2)).astype(jnp.bfloat16)
    return (grad_pair, grad_pair_t, matrices / tokens, vectors / tokens)


def dot_nt(first, second):
    return lax.dot_general(first, second, (((1,), (1,)), ((), ())), preferred_element_type=F32)


def dot_tn(first, second):
    return lax.dot_general(first, second, (((0,), (0,)), ((), ())), preferred_element_type=F32)


def dot_nn(first, second):
    return jnp.dot(first, second, preferred_element_type=F32)


def kernel(
    side,
    tile,
    tokens,
    mask_in,
    pair_in,
    cot_in,
    pw_in,
    ow_in,
    gain_in_ref,
    bias_in_ref,
    gp_ref,
    gpt_ref,
    gm_ref,
    gn_ref,
    mask_ref,
    pair_ref,
    cot_ref,
    pw_ref,
    ow_ref,
    gain_ref,
    bias_ref,
    lb,
    rb,
    pt,
    lf,
    rf,
    dmix,
    mix,
    normal_s,
    spread_s,
    normed_s,
    lin_s,
    open_s,
    gate_s,
    mask_s,
    tnormal_s,
    tspread_s,
    tnormed_s,
    tlin_s,
    topen_s,
    tmask_s,
    dgate_s,
    tback_s,
    sdl,
    sdr,
    rdl,
    rdr,
    early,
    late,
    rearly,
    rlate,
    aearly,
    alate,
    vec,
    rvec,
    in_sem,
    l_send,
    l_recv,
    r_send,
    r_recv,
    p_sem,
    dl_send,
    dl_recv,
    dr_send,
    dr_recv,
    e_send,
    e_recv,
    w_send,
    w_recv,
    ae_send,
    ae_recv,
    aw_send,
    aw_recv,
    v_send,
    v_recv,
):
    r = lax.axis_index("row")
    c = lax.axis_index("col")
    n = side * side
    me = r * side + c
    cells = tile * tile
    erows = early.shape[0] // n
    wrows = late.shape[0] // n

    def at(t):
        return {"row": t // side, "col": lax.rem(t, side)}

    def remote(src, dst, send, recv, row, col):
        return pltpu.make_async_remote_copy(
            src_ref=src,
            dst_ref=dst,
            send_sem=send,
            recv_sem=recv,
            device_id={"row": row, "col": col},
            device_id_type=MESH,
        )

    def others(body):
        def step(p, carry):
            body(lax.rem(me + p, n))
            return carry

        lax.fori_loop(1, n, step, 0)

    loads = [
        pltpu.make_async_copy(src, dst, in_sem.at[at_sem])
        for at_sem, (src, dst) in enumerate(
            (
                (pair_in, pair_ref),
                (pw_in, pw_ref),
                (mask_in, mask_ref),
                (gain_in_ref, gain_ref),
                (bias_in_ref, bias_ref),
                (ow_in, ow_ref),
                (cot_in, cot_ref),
            )
        )
    ]
    for load in loads:
        load.start()
    barrier = pltpu.get_barrier_semaphore()
    others(
        lambda t: pl.semaphore_signal(barrier, inc=1, device_id=at(t), device_id_type=MESH)
    )

    for load in loads:
        load.wait()
    gain_in = gain_ref[0:1, :]
    bias_in = bias_ref[0:1, :]
    gain_mix = gain_ref[1:2, :]
    bias_mix = bias_ref[1:2, :]

    sub = lax.broadcasted_iota(jnp.int32, (tile, 128), 0)
    row_vec = jnp.zeros((tile, 128), F32)
    col_vec = jnp.zeros((tile, 128), F32)
    row_bits = []
    col_bits = []
    for a in range(tile):
        row_bits.append(mask_ref[r * tile + a].astype(F32))
        col_bits.append(mask_ref[c * tile + a].astype(F32))
        row_vec = jnp.where(sub == a, row_bits[a], row_vec)
        col_vec = jnp.where(sub == a, col_bits[a], col_vec)
    for a in range(tile):
        mask_s[a * tile : (a + 1) * tile, :] = col_vec * row_bits[a]
        tmask_s[a * tile : (a + 1) * tile, :] = row_vec * col_bits[a]

    normal, spread = plain_norm(pair_ref[...].reshape(cells, 128))
    normed = (normal * gain_in + bias_in).astype(BF16)
    normal_s[...] = normal
    spread_s[...] = jnp.broadcast_to(spread, (cells, 128))
    normed_s[...] = normed
    pair_mask = mask_s[...]
    lin = dot_nn(normed, pw_ref[0])
    opened = jax.nn.sigmoid(dot_nn(normed, pw_ref[1]))
    lin_s[...] = lin
    open_s[...] = opened
    lb[c] = (opened * lin * pair_mask).astype(BF16).reshape(tile, tile, 128)

    pl.semaphore_wait(barrier, n - 1)

    def left_copy(d):
        return remote(
            lb.at[c], lb.at[c], l_send.at[d], l_recv.at[c], r, lax.rem(c + d, side)
        )

    def right_copy(d):
        return remote(
            rb.at[r], rb.at[r], r_send.at[d], r_recv.at[r], lax.rem(r + d, side), c
        )

    def pair_copy():
        return remote(pair_ref, pt, p_sem.at[0], p_sem.at[1], c, r)

    def left_arrival(b):
        return remote(lb.at[b], lb.at[b], l_send.at[0], l_recv.at[b], r, c)

    def right_arrival(b):
        return remote(rb.at[b], rb.at[b], r_send.at[0], r_recv.at[b], r, c)

    @pl.when(r != c)
    def _():
        pair_copy().start()

    for d in range(1, side):
        left_copy(d).start()

    @pl.when(r == c)
    def _():
        pt[...] = pair_ref[...]

    @pl.when(r != c)
    def _():
        pair_copy().wait_recv()

    tnormal, tspread = plain_norm(pt[...].reshape(cells, 128))
    tnormed = (tnormal * gain_in + bias_in).astype(BF16)
    tnormal_s[...] = tnormal
    tspread_s[...] = jnp.broadcast_to(tspread, (cells, 128))
    tnormed_s[...] = tnormed
    tlin = dot_nn(tnormed, pw_ref[2])
    topen = jax.nn.sigmoid(dot_nn(tnormed, pw_ref[3]))
    tlin_s[...] = tlin
    topen_s[...] = topen
    rb[r] = (topen * tlin * tmask_s[...]).astype(BF16).reshape(tile, tile, 128)
    for d in range(1, side):
        right_copy(d).start()

    gate_s[...] = jax.nn.sigmoid(dot_nn(normed, ow_ref[1]))

    def mix_block(d, accs):
        b = lax.rem(c + d, side)

        @pl.when(d > 0)
        def _():
            left_arrival(b).wait_recv()

        @pl.when(b != r)
        def _():
            right_arrival(b).wait_recv()

        base = pl.multiple_of(b * cells, cells)
        lf[pl.ds(base, cells), :] = lb[b].astype(F32).reshape(cells, 128)
        rf[pl.ds(base, cells), :] = rb[b].astype(F32).reshape(cells, 128)

        def step(k, accs):
            right = rf[pl.ds(base + k, tile, stride=tile), :]
            return tuple(
                accs[i] + lf[pl.ds(base + i * tile + k, 1), :] * right for i in range(tile)
            )

        return lax.fori_loop(0, tile, step, accs)

    zero = jnp.zeros((tile, 128), F32)
    accs = lax.fori_loop(0, side, mix_block, (zero,) * tile)
    for i in range(tile):
        mix[i * tile : (i + 1) * tile, :] = accs[i]

    xhat, mspread = plain_norm(mix[...])
    ynorm = (xhat * gain_mix + bias_mix).astype(BF16)
    upstream = cot_ref[...].reshape(cells, 128).astype(F32)
    gate = gate_s[...]
    d_out = (upstream * gate).astype(BF16)
    d_norm = dot_nt(d_out, ow_ref[0])
    scaled = d_norm * gain_mix
    d_mixing = mspread * (
        scaled
        - jnp.mean(scaled, axis=-1, keepdims=True)
        - xhat * jnp.mean(scaled * xhat, axis=-1, keepdims=True)
    )
    dmix[...] = d_mixing.astype(BF16).astype(F32)
    vec[...] = jnp.zeros_like(vec)
    vec[2:3, :] = jnp.sum(d_norm * xhat, axis=0, keepdims=True)
    vec[3:4, :] = jnp.sum(d_norm, axis=0, keepdims=True)
    outer = dot_nn(ynorm, ow_ref[0])
    d_open = (upstream * outer * gate * (1.0 - gate)).astype(BF16)
    early[0:128, :] = dot_tn(ynorm, d_out).astype(BF16)
    early[128:256, :] = dot_tn(normed_s[...], d_open).astype(BF16)
    dgate_s[...] = dot_nt(d_open, ow_ref[1])

    def chunk_copy(src, rows, dst, send, recv, t):
        return remote(
            src.at[pl.ds(pl.multiple_of(t * rows, rows), rows)],
            dst.at[me],
            send.at[t],
            recv.at[me],
            t // side,
            lax.rem(t, side),
        )

    def chunk_arrival(src, rows, dst, send, recv, t):
        return remote(
            src.at[pl.ds(0, rows)], dst.at[t], send.at[t], recv.at[t], r, c
        )

    others(lambda t: chunk_copy(early, erows, rearly, e_send, e_recv, t).start())
    rearly[me] = early[pl.ds(pl.multiple_of(me * erows, erows), erows), :]

    group = 4

    def left_part(b, out, slot):
        def step(g, carry):
            first = g * group
            sums = [zero] * group
            for j in range(tile):
                right = rf[pl.ds(pl.multiple_of(b * cells + j * tile, tile), tile), :]
                for q in range(group):
                    sums[q] = sums[q] + dmix[pl.ds((first + q) * tile + j, 1), :] * right
            for q in range(group):
                out[slot, first + q] = sums[q].astype(BF16)
            return carry

        lax.fori_loop(0, tile // group, step, 0)

    def right_part(b, out, slot):
        def step(g, carry):
            first = g * group
            sums = [zero] * group
            for i in range(tile):
                left = lf[pl.ds(pl.multiple_of(b * cells + i * tile, tile), tile), :]
                for q in range(group):
                    sums[q] = sums[q] + dmix[pl.ds(i * tile + first + q, 1), :] * left
            for q in range(group):
                out[slot, first + q] = sums[q].astype(BF16)
            return carry

        lax.fori_loop(0, tile // group, step, 0)

    def dl_copy(b):
        return remote(sdl.at[b], rdl.at[c], dl_send.at[b], dl_recv.at[c], r, b)

    def dr_copy(b):
        return remote(sdr.at[b], rdr.at[r], dr_send.at[b], dr_recv.at[r], b, c)

    def dl_arrival(b):
        return remote(sdl.at[b], rdl.at[b], dl_send.at[b], dl_recv.at[b], r, c)

    def dr_arrival(b):
        return remote(sdr.at[b], rdr.at[b], dr_send.at[b], dr_recv.at[b], r, c)

    def part_step(d, carry):
        b = lax.rem(c + d, side)
        left_part(b, sdl, b)
        dl_copy(b).start()
        b = lax.rem(r + d, side)
        right_part(b, sdr, b)
        dr_copy(b).start()
        return carry

    lax.fori_loop(1, side, part_step, 0)
    left_part(c, rdl, c)
    right_part(r, rdr, r)

    others(lambda t: chunk_arrival(early, erows, rearly, e_send, e_recv, t).wait_recv())
    total = rearly[0].astype(F32)
    for s in range(1, n):
        total = total + rearly[s].astype(F32)
    aearly[me] = (total / tokens).astype(BF16)

    def all_copy(buf, send, recv, t):
        return remote(
            buf.at[me], buf.at[me], send.at[t], recv.at[me], t // side, lax.rem(t, side)
        )

    def all_arrival(buf, send, recv, t):
        return remote(buf.at[t], buf.at[t], send.at[t], recv.at[t], r, c)

    others(lambda t: all_copy(aearly, ae_send, ae_recv, t).start())

    def branch_back(received, mask, opened, linear, normed, first):
        total = received[0].astype(F32)
        for s in range(1, side):
            total = total + received[s].astype(F32)
        up = total.astype(BF16).astype(F32).reshape(cells, 128) * mask
        d_lin = (up * opened).astype(BF16)
        d_gate = (up * linear * opened * (1.0 - opened)).astype(BF16)
        late[first * 128 : (first + 1) * 128, :] = dot_tn(normed, d_lin).astype(BF16)
        late[(first + 1) * 128 : (first + 2) * 128, :] = dot_tn(normed, d_gate).astype(BF16)
        return dot_nt(d_lin, pw_ref[first]) + dot_nt(d_gate, pw_ref[first + 1])

    for d in range(1, side):
        dl_arrival(lax.rem(c + d, side)).wait_recv()
    back_left = branch_back(rdl, mask_s[...], open_s[...], lin_s[...], normed_s[...], 0)
    for d in range(1, side):
        dr_arrival(lax.rem(r + d, side)).wait_recv()
    back_right = branch_back(rdr, tmask_s[...], topen_s[...], tlin_s[...], tnormed_s[...], 2)

    others(lambda t: chunk_copy(late, wrows, rlate, w_send, w_recv, t).start())
    rlate[me] = late[pl.ds(pl.multiple_of(me * wrows, wrows), wrows), :]

    main, gain_main, bias_main = norm_back(
        back_left + dgate_s[...], normal_s[...], spread_s[...], gain_in
    )
    turned, gain_side, bias_side = norm_back(
        back_right, tnormal_s[...], tspread_s[...], gain_in
    )
    vec[0:1, :] = (gain_main + gain_side)[None, :]
    vec[1:2, :] = (bias_main + bias_side)[None, :]

    def vec_copy(t):
        return remote(
            vec, rvec.at[me], v_send.at[t], v_recv.at[me], t // side, lax.rem(t, side)
        )

    def vec_arrival(t):
        return remote(vec, rvec.at[t], v_send.at[t], v_recv.at[t], r, c)

    others(lambda t: vec_copy(t).start())
    rvec[me] = vec[...]
    gp_ref[...] = main.astype(BF16).reshape(tile, tile, 128)
    tback_s[...] = turned
    for k in range(tile):
        gpt_ref[k] = tback_s[pl.ds(k, tile, stride=tile), :].astype(BF16)

    others(lambda t: chunk_arrival(late, wrows, rlate, w_send, w_recv, t).wait_recv())
    total = rlate[0].astype(F32)
    for s in range(1, n):
        total = total + rlate[s].astype(F32)
    alate[me] = (total / tokens).astype(BF16)
    others(lambda t: all_copy(alate, aw_send, aw_recv, t).start())

    others(lambda t: vec_arrival(t).wait_recv())
    total = rvec[0]
    for s in range(1, n):
        total = total + rvec[s]
    gn_ref[...] = total[0:4, :] / tokens

    others(lambda t: all_arrival(aearly, ae_send, ae_recv, t).wait_recv())
    gm_ref[4:6] = aearly[...].astype(F32).reshape(2, 128, 128)

    for d in range(1, side):
        left_copy(d).wait_send()
        right_copy(d).wait_send()
        dl_copy(lax.rem(c + d, side)).wait_send()
        dr_copy(lax.rem(r + d, side)).wait_send()

    @pl.when(r != c)
    def _():
        pair_copy().wait_send()

    def sent(t):
        chunk_copy(early, erows, rearly, e_send, e_recv, t).wait_send()
        chunk_copy(late, wrows, rlate, w_send, w_recv, t).wait_send()
        all_copy(aearly, ae_send, ae_recv, t).wait_send()
        vec_copy(t).wait_send()

    others(sent)
    others(lambda t: all_arrival(alate, aw_send, aw_recv, t).wait_recv())
    gm_ref[0:4] = alate[...].astype(F32).reshape(4, 128, 128)
    others(lambda t: all_copy(alate, aw_send, aw_recv, t).wait_send())


def hand_over(*refs):
    sems = refs[8]
    copies = [pltpu.make_async_copy(refs[x], refs[x + 4], sems.at[x]) for x in range(4)]
    for copy in copies:
        copy.start()
    for copy in copies:
        copy.wait()


def fused(side, pair, cotangent, token_mask, proj_weights, out_weights, norm_gains, norm_biases):
    tile = pair.shape[0]
    tokens = token_mask.shape[0]
    n = side * side
    cells = tile * tile
    erows = 256 // n
    wrows = 512 // n
    block = (side, tile, tile, 128)
    wide = pltpu.VMEM((cells, 128), F32)
    slim = pltpu.VMEM((cells, 128), BF16)
    dma = pltpu.SemaphoreType.DMA
    vmem = pl.BlockSpec(memory_space=pltpu.VMEM)
    results = pl.pallas_call(
        functools.partial(kernel, side, tile, tokens),
        out_shape=(
            jax.ShapeDtypeStruct((tile, tile, 128), BF16),
            jax.ShapeDtypeStruct((tile, tile, 128), BF16),
            jax.ShapeDtypeStruct((6, 128, 128), F32),
            jax.ShapeDtypeStruct((4, 128), F32),
        ),
        in_specs=[pl.BlockSpec(memory_space=pl.ANY)] * 7,
        out_specs=(vmem,) * 4,
        scratch_shapes=[
            pltpu.SMEM(token_mask.shape, jnp.int32),
            pltpu.VMEM(pair.shape, BF16),
            pltpu.VMEM(pair.shape, BF16),
            pltpu.VMEM(proj_weights.shape, BF16),
            pltpu.VMEM(out_weights.shape, BF16),
            pltpu.VMEM(norm_gains.shape, F32),
            pltpu.VMEM(norm_biases.shape, F32),
            pltpu.VMEM(block, BF16),
            pltpu.VMEM(block, BF16),
            pltpu.VMEM((tile, tile, 128), BF16),
            pltpu.VMEM((side * cells, 128), F32),
            pltpu.VMEM((side * cells, 128), F32),
            wide,
            wide,
            wide,
            wide,
            slim,
            wide,
            wide,
            wide,
            wide,
            wide,
            wide,
            slim,
            wide,
            wide,
            wide,
            wide,
            wide,
            pltpu.VMEM(block, BF16),
            pltpu.VMEM(block, BF16),
            pltpu.VMEM(block, BF16),
            pltpu.VMEM(block, BF16),
            pltpu.VMEM((256, 128), BF16),
            pltpu.VMEM((512, 128), BF16),
            pltpu.VMEM((n, erows, 128), BF16),
            pltpu.VMEM((n, wrows, 128), BF16),
            pltpu.VMEM((n, erows, 128), BF16),
            pltpu.VMEM((n, wrows, 128), BF16),
            pltpu.VMEM((8, 128), F32),
            pltpu.VMEM((n, 8, 128), F32),
            dma((7,)),
            dma((side,)),
            dma((side,)),
            dma((side,)),
            dma((side,)),
            dma((2,)),
            dma((side,)),
            dma((side,)),
            dma((side,)),
            dma((side,)),
        ]
        + [dma((n,))] * 10,
        compiler_params=pltpu.CompilerParams(
            collective_id=0, has_side_effects=True, vmem_limit_bytes=40 * 1024 * 1024
        ),
    )(token_mask, pair, cotangent, proj_weights, out_weights, norm_gains, norm_biases)
    anywhere = pl.BlockSpec(memory_space=pl.ANY)
    return pl.pallas_call(
        hand_over,
        out_shape=tuple(jax.ShapeDtypeStruct(x.shape, x.dtype) for x in results),
        in_specs=[anywhere] * 4,
        out_specs=(anywhere,) * 4,
        scratch_shapes=[dma((4,))],
    )(*results)


def device_program(*args):
    rows, cols = lax.axis_size("row"), lax.axis_size("col")
    pair = args[0]
    square = rows == cols and pair.shape[0] == pair.shape[1] == 16
    if square and 256 % (16 * rows * cols) == 0 and pair.shape[2] == 128:
        return fused(rows, *args)
    return per_device(*args)


def solution(mesh):
    in_specs = (
        P(("grp", "row"), "col", None),
        P(("grp", "row"), "col", None),
        P("grp"),
        P(),
        P(),
        P(),
        P(),
    )
    out_specs = (
        P(("grp", "row"), "col", None),
        P(("grp", "row"), "col", None),
        P("grp", None, None),
        P("grp", None),
    )
    return jax.shard_map(
        device_program, mesh=mesh, in_specs=in_specs, out_specs=out_specs, check_vma=False
    )
```

```python
import functools

import jax
import jax.numpy as jnp
from jax import lax
from jax.experimental import pallas as pl
from jax.experimental.pallas import tpu as pltpu
from jax.sharding import PartitionSpec as P

MESH = pl.DeviceIdType.MESH
F32 = jnp.float32
BF16 = jnp.bfloat16

EPS = 1e-05


def spread_2(x, axis, root):
    mine = lax.axis_index(axis) == root
    return lax.psum(jnp.where(mine, x, jnp.zeros_like(x)), axis)


def plain_norm(source):
    source = source.astype(jnp.float32)
    center = source - jnp.mean(source, axis=-1, keepdims=True)
    spread = lax.rsqrt(jnp.mean(center * center, axis=-1, keepdims=True) + EPS)
    return (center * spread, spread)


def matmul(operand, weight):
    extent = operand.shape
    flattened = operand.reshape(-1, extent[-1])
    result = jnp.dot(flattened, weight, preferred_element_type=jnp.float32)
    return result.reshape(extent[:-1] + (weight.shape[-1],))


def column_sum(values):
    return jnp.sum(values.reshape(-1, values.shape[-1]), axis=0)


def outer_sum(first, second):
    return jnp.dot(
        first.reshape(-1, first.shape[-1]).T,
        second.reshape(-1, second.shape[-1]),
        preferred_element_type=jnp.float32,
    )


def project(normed, weight, gate_weight, pair_mask):
    linear = matmul(normed, weight)
    opened = jax.nn.sigmoid(matmul(normed, gate_weight))
    return ((opened * linear * pair_mask).astype(jnp.bfloat16), linear, opened)


def project_back(d_proj, normed, linear, opened, pair_mask, weight, gate_weight):
    upstream = d_proj.astype(jnp.float32) * pair_mask
    d_linear = (upstream * opened).astype(jnp.bfloat16)
    d_opened = (upstream * linear * opened * (1.0 - opened)).astype(jnp.bfloat16)
    grad_weight = outer_sum(normed, d_linear)
    grad_gate = outer_sum(normed, d_opened)
    returned = matmul(d_linear, weight.T) + matmul(d_opened, gate_weight.T)
    return (returned, grad_weight, grad_gate)


def norm_back(upstream, normal, spread, gain_vec):
    scaled_up = upstream * gain_vec
    returned = spread * (
        scaled_up
        - jnp.mean(scaled_up, axis=-1, keepdims=True)
        - normal * jnp.mean(scaled_up * normal, axis=-1, keepdims=True)
    )
    return (returned, column_sum(upstream * normal), column_sum(upstream))


def output_back(mixing, normed, cotangent, out_weight, gate_weight, gain_vec, bias_vec):
    normal, spread = plain_norm(mixing)
    ynorm = (normal * gain_vec + bias_vec).astype(jnp.bfloat16)
    outer = matmul(ynorm, out_weight)
    opened = jax.nn.sigmoid(matmul(normed, gate_weight))
    upstream = cotangent.astype(jnp.float32)
    d_out = (upstream * opened).astype(jnp.bfloat16)
    d_opened = (upstream * outer * opened * (1.0 - opened)).astype(jnp.bfloat16)
    grad_out = outer_sum(ynorm, d_out)
    grad_gate = outer_sum(normed, d_opened)
    d_norm = matmul(d_out, out_weight.T)
    d_mixing, grad_gain, grad_bias = norm_back(d_norm, normal, spread, gain_vec)
    return (
        d_mixing.astype(jnp.bfloat16),
        matmul(d_opened, gate_weight.T),
        grad_out,
        grad_gate,
        grad_gain,
        grad_bias,
    )


def take_cols(values, offset, amount):
    return lax.dynamic_slice_in_dim(values, offset, amount, 1)


def per_device(pair, cotangent, token_mask, proj_weights, out_weights, norm_gains, norm_biases):
    tile_rows = pair.shape[0]
    tile_cols = pair.shape[1]
    tokens = token_mask.shape[0]
    repeat_count = lax.axis_size("row") // lax.axis_size("col")
    row_index = lax.axis_index("row")
    col_index = lax.axis_index("col")
    presence = token_mask.astype(jnp.float32)
    row_presence = lax.dynamic_slice_in_dim(presence, row_index * tile_rows, tile_rows)
    col_presence = lax.dynamic_slice_in_dim(presence, col_index * tile_cols, tile_cols)
    tile_mask = (row_presence[:, None] * col_presence[None, :])[:, :, None]
    gain_in = norm_gains[0]
    bias_in = norm_biases[0]
    strip = lax.all_gather(pair, "col", axis=1, tiled=True)
    strip_normal, strip_spread = plain_norm(strip)
    strip_normed = (strip_normal * gain_in + bias_in).astype(jnp.bfloat16)
    strip_mask = (row_presence[:, None] * presence[None, :])[:, :, None]
    left_rows, strip_lin, strip_open = project(
        strip_normed, proj_weights[0], proj_weights[1], strip_mask
    )
    first_col = col_index * tile_cols
    normal = take_cols(strip_normal, first_col, tile_cols)
    spread = take_cols(strip_spread, first_col, tile_cols)
    normed = take_cols(strip_normed, first_col, tile_cols)
    left_lin = take_cols(strip_lin, first_col, tile_cols)
    left_open = take_cols(strip_open, first_col, tile_cols)
    first_key = row_index * tile_rows
    side_mask = (col_presence[:, None] * row_presence[None, :])[:, :, None]
    pieces = []
    for offset in range(repeat_count):
        pieces.append(spread_2(strip, "row", col_index * repeat_count + offset))
    column_pairs = jnp.concatenate(pieces, axis=0)
    right_normal, right_spread = plain_norm(column_pairs)
    right_normed = (right_normal * gain_in + bias_in).astype(jnp.bfloat16)
    right_mask = (col_presence[:, None] * presence[None, :])[:, :, None]
    right_rows, right_lin, right_open = project(
        right_normed, proj_weights[2], proj_weights[3], right_mask
    )
    side_normal = take_cols(right_normal, first_key, tile_rows)
    side_spread = take_cols(right_spread, first_key, tile_rows)
    side_normed = take_cols(right_normed, first_key, tile_rows)
    side_lin = take_cols(right_lin, first_key, tile_rows)
    side_open = take_cols(right_open, first_key, tile_rows)
    mixing = jnp.einsum("ikh,jkh->ijh", left_rows, right_rows, preferred_element_type=jnp.float32)
    d_mixing, d_gate_in, grad_out, grad_gate, grad_gain, grad_bias = output_back(
        mixing, normed, cotangent, out_weights[0], out_weights[1], norm_gains[1], norm_biases[1]
    )
    portion = take_cols(right_rows, jnp.int32(0), lax.axis_size("col") * tile_cols)
    d_left = lax.psum_scatter(
        jnp.einsum("ijh,jkh->kih", d_mixing, portion, preferred_element_type=jnp.float32).astype(
            jnp.bfloat16
        ),
        "col",
        scatter_dimension=0,
        tiled=True,
    ).astype(jnp.float32)
    d_left = jnp.transpose(d_left, (1, 0, 2)).astype(jnp.bfloat16)
    portion = take_cols(left_rows, jnp.int32(0), lax.axis_size("row") * tile_rows)
    d_right = lax.psum_scatter(
        jnp.einsum("ijh,ikh->kjh", d_mixing, portion, preferred_element_type=jnp.float32).astype(
            jnp.bfloat16
        ),
        "row",
        scatter_dimension=0,
        tiled=True,
    ).astype(jnp.float32)
    d_right = jnp.transpose(d_right, (1, 0, 2)).astype(jnp.bfloat16)
    back_left, grad_lw, grad_lg = project_back(
        d_left, normed, left_lin, left_open, tile_mask, proj_weights[0], proj_weights[1]
    )
    back_right, grad_rw, grad_rg = project_back(
        d_right, side_normed, side_lin, side_open, side_mask, proj_weights[2], proj_weights[3]
    )
    main_back, gain_main, bias_main = norm_back(back_left + d_gate_in, normal, spread, gain_in)
    side_back, gain_side, bias_side = norm_back(back_right, side_normal, side_spread, gain_in)
    matrices = jnp.stack([grad_lw, grad_lg, grad_rw, grad_rg, grad_out, grad_gate])
    vectors = jnp.stack([gain_main + gain_side, bias_main + bias_side, grad_gain, grad_bias])
    matrices, vectors = lax.psum((matrices, vectors), ("row", "col"))
    grad_pair = main_back.astype(jnp.bfloat16)
    grad_pair_t = jnp.transpose(side_back, (1, 0, 2)).astype(jnp.bfloat16)
    return (grad_pair, grad_pair_t, matrices / tokens, vectors / tokens)


def dot_nt(first, second):
    return lax.dot_general(first, second, (((1,), (1,)), ((), ())), preferred_element_type=F32)


def dot_tn(first, second):
    return lax.dot_general(first, second, (((0,), (0,)), ((), ())), preferred_element_type=F32)


def dot_nn(first, second):
    return jnp.dot(first, second, preferred_element_type=F32)


def kernel(
    side,
    tile,
    tokens,
    mask_in,
    pair_in,
    cot_in,
    pw_in,
    ow_in,
    gain_in_ref,
    bias_in_ref,
    gp_ref,
    gpt_ref,
    gm_ref,
    gn_ref,
    mask_ref,
    pair_ref,
    cot_ref,
    pw_ref,
    ow_ref,
    gain_ref,
    bias_ref,
    lb,
    rb,
    pt,
    lf,
    rf,
    dmix,
    mix,
    normal_s,
    spread_s,
    normed_s,
    lin_s,
    open_s,
    gate_s,
    mask_s,
    tnormal_s,
    tspread_s,
    tnormed_s,
    tlin_s,
    topen_s,
    tmask_s,
    dgate_s,
    tback_s,
    sdl,
    sdr,
    rdl,
    rdr,
    early,
    late,
    rearly,
    rlate,
    aearly,
    alate,
    vec,
    rvec,
    in_sem,
    l_send,
    l_recv,
    r_send,
    r_recv,
    p_sem,
    dl_send,
    dl_recv,
    dr_send,
    dr_recv,
    e_send,
    e_recv,
    w_send,
    w_recv,
    ae_send,
    ae_recv,
    aw_send,
    aw_recv,
    v_send,
    v_recv,
):
    r = lax.axis_index("row")
    c = lax.axis_index("col")
    n = side * side
    me = r * side + c
    cells = tile * tile
    erows = early.shape[0] // n
    wrows = late.shape[0] // n

    def at(t):
        return {"row": t // side, "col": lax.rem(t, side)}

    def remote(src, dst, send, recv, row, col):
        return pltpu.make_async_remote_copy(
            src_ref=src,
            dst_ref=dst,
            send_sem=send,
            recv_sem=recv,
            device_id={"row": row, "col": col},
            device_id_type=MESH,
        )

    def others(body):
        def step(p, carry):
            body(lax.rem(me + p, n))
            return carry

        lax.fori_loop(1, n, step, 0)

    loads = [
        pltpu.make_async_copy(src, dst, in_sem.at[at_sem])
        for at_sem, (src, dst) in enumerate(
            (
                (pair_in, pair_ref),
                (pw_in, pw_ref),
                (mask_in, mask_ref),
                (gain_in_ref, gain_ref),
                (bias_in_ref, bias_ref),
                (ow_in, ow_ref),
                (cot_in, cot_ref),
            )
        )
    ]
    for load in loads:
        load.start()
    barrier = pltpu.get_barrier_semaphore()
    others(
        lambda t: pl.semaphore_signal(barrier, inc=1, device_id=at(t), device_id_type=MESH)
    )

    for load in loads:
        load.wait()
    gain_in = gain_ref[0:1, :]
    bias_in = bias_ref[0:1, :]
    gain_mix = gain_ref[1:2, :]
    bias_mix = bias_ref[1:2, :]

    sub = lax.broadcasted_iota(jnp.int32, (tile, 128), 0)
    row_vec = jnp.zeros((tile, 128), F32)
    col_vec = jnp.zeros((tile, 128), F32)
    row_bits = []
    col_bits = []
    for a in range(tile):
        row_bits.append(mask_ref[r * tile + a].astype(F32))
        col_bits.append(mask_ref[c * tile + a].astype(F32))
        row_vec = jnp.where(sub == a, row_bits[a], row_vec)
        col_vec = jnp.where(sub == a, col_bits[a], col_vec)
    for a in range(tile):
        mask_s[a * tile : (a + 1) * tile, :] = col_vec * row_bits[a]
        tmask_s[a * tile : (a + 1) * tile, :] = row_vec * col_bits[a]

    normal, spread = plain_norm(pair_ref[...].reshape(cells, 128))
    normed = (normal * gain_in + bias_in).astype(BF16)
    normal_s[...] = normal
    spread_s[...] = jnp.broadcast_to(spread, (cells, 128))
    normed_s[...] = normed
    pair_mask = mask_s[...]
    lin = dot_nn(normed, pw_ref[0])
    opened = jax.nn.sigmoid(dot_nn(normed, pw_ref[1]))
    lin_s[...] = lin
    open_s[...] = opened
    lb[c] = (opened * lin * pair_mask).astype(BF16).reshape(tile, tile, 128)

    pl.semaphore_wait(barrier, n - 1)

    def left_copy(d):
        return remote(
            lb.at[c], lb.at[c], l_send.at[d], l_recv.at[c], r, lax.rem(c + d, side)
        )

    def right_copy(d):
        return remote(
            rb.at[r], rb.at[r], r_send.at[d], r_recv.at[r], lax.rem(r + d, side), c
        )

    def pair_copy():
        return remote(pair_ref, pt, p_sem.at[0], p_sem.at[1], c, r)

    def left_arrival(b):
        return remote(lb.at[b], lb.at[b], l_send.at[0], l_recv.at[b], r, c)

    def right_arrival(b):
        return remote(rb.at[b], rb.at[b], r_send.at[0], r_recv.at[b], r, c)

    @pl.when(r != c)
    def _():
        pair_copy().start()

    for d in range(1, side):
        left_copy(d).start()

    @pl.when(r == c)
    def _():
        pt[...] = pair_ref[...]

    @pl.when(r != c)
    def _():
        pair_copy().wait_recv()

    tnormal, tspread = plain_norm(pt[...].reshape(cells, 128))
    tnormed = (tnormal * gain_in + bias_in).astype(BF16)
    tnormal_s[...] = tnormal
    tspread_s[...] = jnp.broadcast_to(tspread, (cells, 128))
    tnormed_s[...] = tnormed
    tlin = dot_nn(tnormed, pw_ref[2])
    topen = jax.nn.sigmoid(dot_nn(tnormed, pw_ref[3]))
    tlin_s[...] = tlin
    topen_s[...] = topen
    rb[r] = (topen * tlin * tmask_s[...]).astype(BF16).reshape(tile, tile, 128)
    for d in range(1, side):
        right_copy(d).start()

    gate_s[...] = jax.nn.sigmoid(dot_nn(normed, ow_ref[1]))

    def mix_block(d, accs):
        b = lax.rem(c + d, side)

        @pl.when(d > 0)
        def _():
            left_arrival(b).wait_recv()

        @pl.when(b != r)
        def _():
            right_arrival(b).wait_recv()

        base = pl.multiple_of(b * cells, cells)
        lf[pl.ds(base, cells), :] = lb[b].astype(F32).reshape(cells, 128)
        rf[pl.ds(base, cells), :] = rb[b].astype(F32).reshape(cells, 128)

        def step(k, accs):
            right = rf[pl.ds(base + k, tile, stride=tile), :]
            return tuple(
                accs[i] + lf[pl.ds(base + i * tile + k, 1), :] * right for i in range(tile)
            )

        return lax.fori_loop(0, tile, step, accs)

    zero = jnp.zeros((tile, 128), F32)
    accs = lax.fori_loop(0, side, mix_block, (zero,) * tile)
    for i in range(tile):
        mix[i * tile : (i + 1) * tile, :] = accs[i]

    xhat, mspread = plain_norm(mix[...])
    ynorm = (xhat * gain_mix + bias_mix).astype(BF16)
    upstream = cot_ref[...].reshape(cells, 128).astype(F32)
    gate = gate_s[...]
    d_out = (upstream * gate).astype(BF16)
    d_norm = dot_nt(d_out, ow_ref[0])
    scaled = d_norm * gain_mix
    d_mixing = mspread * (
        scaled
        - jnp.mean(scaled, axis=-1, keepdims=True)
        - xhat * jnp.mean(scaled * xhat, axis=-1, keepdims=True)
    )
    dmix[...] = d_mixing.astype(BF16).astype(F32)
    vec[...] = jnp.zeros_like(vec)
    vec[2:3, :] = jnp.sum(d_norm * xhat, axis=0, keepdims=True)
    vec[3:4, :] = jnp.sum(d_norm, axis=0, keepdims=True)
    outer = dot_nn(ynorm, ow_ref[0])
    d_open = (upstream * outer * gate * (1.0 - gate)).astype(BF16)
    early[0:128, :] = dot_tn(ynorm, d_out).astype(BF16)
    early[128:256, :] = dot_tn(normed_s[...], d_open).astype(BF16)
    dgate_s[...] = dot_nt(d_open, ow_ref[1])

    def chunk_copy(src, rows, dst, send, recv, t):
        return remote(
            src.at[pl.ds(pl.multiple_of(t * rows, rows), rows)],
            dst.at[me],
            send.at[t],
            recv.at[me],
            t // side,
            lax.rem(t, side),
        )

    def chunk_arrival(src, rows, dst, send, recv, t):
        return remote(
            src.at[pl.ds(0, rows)], dst.at[t], send.at[t], recv.at[t], r, c
        )

    others(lambda t: chunk_copy(early, erows, rearly, e_send, e_recv, t).start())
    rearly[me] = early[pl.ds(pl.multiple_of(me * erows, erows), erows), :]

    group = 4

    def left_part(b, out, slot):
        def step(g, carry):
            first = g * group
            sums = [zero] * group
            for j in range(tile):
                right = rf[pl.ds(pl.multiple_of(b * cells + j * tile, tile), tile), :]
                for q in range(group):
                    sums[q] = sums[q] + dmix[pl.ds((first + q) * tile + j, 1), :] * right
            for q in range(group):
                out[slot, first + q] = sums[q].astype(BF16)
            return carry

        lax.fori_loop(0, tile // group, step, 0)

    def right_part(b, out, slot):
        def step(g, carry):
            first = g * group
            sums = [zero] * group
            for i in range(tile):
                left = lf[pl.ds(pl.multiple_of(b * cells + i * tile, tile), tile), :]
                for q in range(group):
                    sums[q] = sums[q] + dmix[pl.ds(i * tile + first + q, 1), :] * left
            for q in range(group):
                out[slot, first + q] = sums[q].astype(BF16)
            return carry

        lax.fori_loop(0, tile // group, step, 0)

    def dl_copy(b):
        return remote(sdl.at[b], rdl.at[c], dl_send.at[b], dl_recv.at[c], r, b)

    def dr_copy(b):
        return remote(sdr.at[b], rdr.at[r], dr_send.at[b], dr_recv.at[r], b, c)

    def dl_arrival(b):
        return remote(sdl.at[b], rdl.at[b], dl_send.at[b], dl_recv.at[b], r, c)

    def dr_arrival(b):
        return remote(sdr.at[b], rdr.at[b], dr_send.at[b], dr_recv.at[b], r, c)

    def part_step(d, carry):
        b = lax.rem(c + d, side)
        left_part(b, sdl, b)
        dl_copy(b).start()
        b = lax.rem(r + d, side)
        right_part(b, sdr, b)
        dr_copy(b).start()
        return carry

    lax.fori_loop(1, side, part_step, 0)
    left_part(c, rdl, c)
    right_part(r, rdr, r)

    others(lambda t: chunk_arrival(early, erows, rearly, e_send, e_recv, t).wait_recv())
    total = rearly[0].astype(F32)
    for s in range(1, n):
        total = total + rearly[s].astype(F32)
    aearly[me] = (total / tokens).astype(BF16)

    def all_copy(buf, send, recv, t):
        return remote(
            buf.at[me], buf.at[me], send.at[t], recv.at[me], t // side, lax.rem(t, side)
        )

    def all_arrival(buf, send, recv, t):
        return remote(buf.at[t], buf.at[t], send.at[t], recv.at[t], r, c)

    others(lambda t: all_copy(aearly, ae_send, ae_recv, t).start())

    def branch_back(received, mask, opened, linear, normed, first):
        total = received[0].astype(F32)
        for s in range(1, side):
            total = total + received[s].astype(F32)
        up = total.astype(BF16).astype(F32).reshape(cells, 128) * mask
        d_lin = (up * opened).astype(BF16)
        d_gate = (up * linear * opened * (1.0 - opened)).astype(BF16)
        late[first * 128 : (first + 1) * 128, :] = dot_tn(normed, d_lin).astype(BF16)
        late[(first + 1) * 128 : (first + 2) * 128, :] = dot_tn(normed, d_gate).astype(BF16)
        return dot_nt(d_lin, pw_ref[first]) + dot_nt(d_gate, pw_ref[first + 1])

    for d in range(1, side):
        dl_arrival(lax.rem(c + d, side)).wait_recv()
    back_left = branch_back(rdl, mask_s[...], open_s[...], lin_s[...], normed_s[...], 0)
    for d in range(1, side):
        dr_arrival(lax.rem(r + d, side)).wait_recv()
    back_right = branch_back(rdr, tmask_s[...], topen_s[...], tlin_s[...], tnormed_s[...], 2)

    others(lambda t: chunk_copy(late, wrows, rlate, w_send, w_recv, t).start())
    rlate[me] = late[pl.ds(pl.multiple_of(me * wrows, wrows), wrows), :]

    main, gain_main, bias_main = norm_back(
        back_left + dgate_s[...], normal_s[...], spread_s[...], gain_in
    )
    turned, gain_side, bias_side = norm_back(
        back_right, tnormal_s[...], tspread_s[...], gain_in
    )
    vec[0:1, :] = (gain_main + gain_side)[None, :]
    vec[1:2, :] = (bias_main + bias_side)[None, :]

    def vec_copy(t):
        return remote(
            vec, rvec.at[me], v_send.at[t], v_recv.at[me], t // side, lax.rem(t, side)
        )

    def vec_arrival(t):
        return remote(vec, rvec.at[t], v_send.at[t], v_recv.at[t], r, c)

    others(lambda t: vec_copy(t).start())
    rvec[me] = vec[...]
    gp_ref[...] = main.astype(BF16).reshape(tile, tile, 128)
    tback_s[...] = turned
    for k in range(tile):
        gpt_ref[k] = tback_s[pl.ds(k, tile, stride=tile), :].astype(BF16)

    others(lambda t: chunk_arrival(late, wrows, rlate, w_send, w_recv, t).wait_recv())
    total = rlate[0].astype(F32)
    for s in range(1, n):
        total = total + rlate[s].astype(F32)
    alate[me] = (total / tokens).astype(BF16)
    others(lambda t: all_copy(alate, aw_send, aw_recv, t).start())

    others(lambda t: vec_arrival(t).wait_recv())
    total = rvec[0]
    for s in range(1, n):
        total = total + rvec[s]
    gn_ref[...] = total[0:4, :] / tokens

    others(lambda t: all_arrival(aearly, ae_send, ae_recv, t).wait_recv())
    gm_ref[4:6] = aearly[...].astype(F32).reshape(2, 128, 128)

    for d in range(1, side):
        left_copy(d).wait_send()
        right_copy(d).wait_send()
        dl_copy(lax.rem(c + d, side)).wait_send()
        dr_copy(lax.rem(r + d, side)).wait_send()

    @pl.when(r != c)
    def _():
        pair_copy().wait_send()

    def sent(t):
        chunk_copy(early, erows, rearly, e_send, e_recv, t).wait_send()
        chunk_copy(late, wrows, rlate, w_send, w_recv, t).wait_send()
        all_copy(aearly, ae_send, ae_recv, t).wait_send()
        vec_copy(t).wait_send()

    others(sent)
    others(lambda t: all_arrival(alate, aw_send, aw_recv, t).wait_recv())
    gm_ref[0:4] = alate[...].astype(F32).reshape(4, 128, 128)
    others(lambda t: all_copy(alate, aw_send, aw_recv, t).wait_send())


def hand_over(*refs):
    sems = refs[8]
    copies = [pltpu.make_async_copy(refs[x], refs[x + 4], sems.at[x]) for x in range(4)]
    for copy in copies:
        copy.start()
    for copy in copies:
        copy.wait()


def fused(side, pair, cotangent, token_mask, proj_weights, out_weights, norm_gains, norm_biases):
    tile = pair.shape[0]
    tokens = token_mask.shape[0]
    n = side * side
    cells = tile * tile
    erows = 256 // n
    wrows = 512 // n
    block = (side, tile, tile, 128)
    wide = pltpu.VMEM((cells, 128), F32)
    slim = pltpu.VMEM((cells, 128), BF16)
    dma = pltpu.SemaphoreType.DMA
    vmem = pl.BlockSpec(memory_space=pltpu.VMEM)
    results = pl.pallas_call(
        functools.partial(kernel, side, tile, tokens),
        out_shape=(
            jax.ShapeDtypeStruct((tile, tile, 128), BF16),
            jax.ShapeDtypeStruct((tile, tile, 128), BF16),
            jax.ShapeDtypeStruct((6, 128, 128), F32),
            jax.ShapeDtypeStruct((4, 128), F32),
        ),
        in_specs=[pl.BlockSpec(memory_space=pltpu.HBM)] * 7,
        out_specs=(vmem,) * 4,
        scratch_shapes=[
            pltpu.SMEM(token_mask.shape, jnp.int32),
            pltpu.VMEM(pair.shape, BF16),
            pltpu.VMEM(pair.shape, BF16),
            pltpu.VMEM(proj_weights.shape, BF16),
            pltpu.VMEM(out_weights.shape, BF16),
            pltpu.VMEM(norm_gains.shape, F32),
            pltpu.VMEM(norm_biases.shape, F32),
            pltpu.VMEM(block, BF16),
            pltpu.VMEM(block, BF16),
            pltpu.VMEM((tile, tile, 128), BF16),
            pltpu.VMEM((side * cells, 128), F32),
            pltpu.VMEM((side * cells, 128), F32),
            wide,
            wide,
            wide,
            wide,
            slim,
            wide,
            wide,
            wide,
            wide,
            wide,
            wide,
            slim,
            wide,
            wide,
            wide,
            wide,
            wide,
            pltpu.VMEM(block, BF16),
            pltpu.VMEM(block, BF16),
            pltpu.VMEM(block, BF16),
            pltpu.VMEM(block, BF16),
            pltpu.VMEM((256, 128), BF16),
            pltpu.VMEM((512, 128), BF16),
            pltpu.VMEM((n, erows, 128), BF16),
            pltpu.VMEM((n, wrows, 128), BF16),
            pltpu.VMEM((n, erows, 128), BF16),
            pltpu.VMEM((n, wrows, 128), BF16),
            pltpu.VMEM((8, 128), F32),
            pltpu.VMEM((n, 8, 128), F32),
            dma((7,)),
            dma((side,)),
            dma((side,)),
            dma((side,)),
            dma((side,)),
            dma((2,)),
            dma((side,)),
            dma((side,)),
            dma((side,)),
            dma((side,)),
        ]
        + [dma((n,))] * 10,
        compiler_params=pltpu.CompilerParams(
            collective_id=0, has_side_effects=True, vmem_limit_bytes=63 * 1024 * 1024
        ),
    )(token_mask, pair, cotangent, proj_weights, out_weights, norm_gains, norm_biases)
    main = pl.BlockSpec(memory_space=pltpu.HBM)
    return pl.pallas_call(
        hand_over,
        out_shape=tuple(jax.ShapeDtypeStruct(x.shape, x.dtype) for x in results),
        in_specs=[vmem] * 4,
        out_specs=(main,) * 4,
        scratch_shapes=[dma((4,))],
    )(*results)


def device_program(*args):
    rows, cols = lax.axis_size("row"), lax.axis_size("col")
    pair = args[0]
    square = rows == cols and pair.shape[0] == pair.shape[1] == 16
    if square and 256 % (16 * rows * cols) == 0 and pair.shape[2] == 128:
        return fused(rows, *args)
    return per_device(*args)


def solution(mesh):
    in_specs = (
        P(("grp", "row"), "col", None),
        P(("grp", "row"), "col", None),
        P("grp"),
        P(),
        P(),
        P(),
        P(),
    )
    out_specs = (
        P(("grp", "row"), "col", None),
        P(("grp", "row"), "col", None),
        P("grp", None, None),
        P("grp", None),
    )
    return jax.shard_map(
        device_program, mesh=mesh, in_specs=in_specs, out_specs=out_specs, check_vma=False
    )
```

```python
import functools

import jax
import jax.numpy as jnp
from jax import lax
from jax.experimental import pallas as pl
from jax.experimental.pallas import tpu as pltpu
from jax.sharding import PartitionSpec as P

MESH = pl.DeviceIdType.MESH
F32 = jnp.float32
BF16 = jnp.bfloat16

EPS = 1e-05


def spread_2(x, axis, root):
    mine = lax.axis_index(axis) == root
    return lax.psum(jnp.where(mine, x, jnp.zeros_like(x)), axis)


def plain_norm(source):
    source = source.astype(jnp.float32)
    center = source - jnp.mean(source, axis=-1, keepdims=True)
    spread = lax.rsqrt(jnp.mean(center * center, axis=-1, keepdims=True) + EPS)
    return (center * spread, spread)


def matmul(operand, weight):
    extent = operand.shape
    flattened = operand.reshape(-1, extent[-1])
    result = jnp.dot(flattened, weight, preferred_element_type=jnp.float32)
    return result.reshape(extent[:-1] + (weight.shape[-1],))


def column_sum(values):
    return jnp.sum(values.reshape(-1, values.shape[-1]), axis=0)


def outer_sum(first, second):
    return jnp.dot(
        first.reshape(-1, first.shape[-1]).T,
        second.reshape(-1, second.shape[-1]),
        preferred_element_type=jnp.float32,
    )


def project(normed, weight, gate_weight, pair_mask):
    linear = matmul(normed, weight)
    opened = jax.nn.sigmoid(matmul(normed, gate_weight))
    return ((opened * linear * pair_mask).astype(jnp.bfloat16), linear, opened)


def project_back(d_proj, normed, linear, opened, pair_mask, weight, gate_weight):
    upstream = d_proj.astype(jnp.float32) * pair_mask
    d_linear = (upstream * opened).astype(jnp.bfloat16)
    d_opened = (upstream * linear * opened * (1.0 - opened)).astype(jnp.bfloat16)
    grad_weight = outer_sum(normed, d_linear)
    grad_gate = outer_sum(normed, d_opened)
    returned = matmul(d_linear, weight.T) + matmul(d_opened, gate_weight.T)
    return (returned, grad_weight, grad_gate)


def norm_back(upstream, normal, spread, gain_vec):
    scaled_up = upstream * gain_vec
    returned = spread * (
        scaled_up
        - jnp.mean(scaled_up, axis=-1, keepdims=True)
        - normal * jnp.mean(scaled_up * normal, axis=-1, keepdims=True)
    )
    return (returned, column_sum(upstream * normal), column_sum(upstream))


def output_back(mixing, normed, cotangent, out_weight, gate_weight, gain_vec, bias_vec):
    normal, spread = plain_norm(mixing)
    ynorm = (normal * gain_vec + bias_vec).astype(jnp.bfloat16)
    outer = matmul(ynorm, out_weight)
    opened = jax.nn.sigmoid(matmul(normed, gate_weight))
    upstream = cotangent.astype(jnp.float32)
    d_out = (upstream * opened).astype(jnp.bfloat16)
    d_opened = (upstream * outer * opened * (1.0 - opened)).astype(jnp.bfloat16)
    grad_out = outer_sum(ynorm, d_out)
    grad_gate = outer_sum(normed, d_opened)
    d_norm = matmul(d_out, out_weight.T)
    d_mixing, grad_gain, grad_bias = norm_back(d_norm, normal, spread, gain_vec)
    return (
        d_mixing.astype(jnp.bfloat16),
        matmul(d_opened, gate_weight.T),
        grad_out,
        grad_gate,
        grad_gain,
        grad_bias,
    )


def take_cols(values, offset, amount):
    return lax.dynamic_slice_in_dim(values, offset, amount, 1)


def per_device(pair, cotangent, token_mask, proj_weights, out_weights, norm_gains, norm_biases):
    tile_rows = pair.shape[0]
    tile_cols = pair.shape[1]
    tokens = token_mask.shape[0]
    repeat_count = lax.axis_size("row") // lax.axis_size("col")
    row_index = lax.axis_index("row")
    col_index = lax.axis_index("col")
    presence = token_mask.astype(jnp.float32)
    row_presence = lax.dynamic_slice_in_dim(presence, row_index * tile_rows, tile_rows)
    col_presence = lax.dynamic_slice_in_dim(presence, col_index * tile_cols, tile_cols)
    tile_mask = (row_presence[:, None] * col_presence[None, :])[:, :, None]
    gain_in = norm_gains[0]
    bias_in = norm_biases[0]
    strip = lax.all_gather(pair, "col", axis=1, tiled=True)
    strip_normal, strip_spread = plain_norm(strip)
    strip_normed = (strip_normal * gain_in + bias_in).astype(jnp.bfloat16)
    strip_mask = (row_presence[:, None] * presence[None, :])[:, :, None]
    left_rows, strip_lin, strip_open = project(
        strip_normed, proj_weights[0], proj_weights[1], strip_mask
    )
    first_col = col_index * tile_cols
    normal = take_cols(strip_normal, first_col, tile_cols)
    spread = take_cols(strip_spread, first_col, tile_cols)
    normed = take_cols(strip_normed, first_col, tile_cols)
    left_lin = take_cols(strip_lin, first_col, tile_cols)
    left_open = take_cols(strip_open, first_col, tile_cols)
    first_key = row_index * tile_rows
    side_mask = (col_presence[:, None] * row_presence[None, :])[:, :, None]
    pieces = []
    for offset in range(repeat_count):
        pieces.append(spread_2(strip, "row", col_index * repeat_count + offset))
    column_pairs = jnp.concatenate(pieces, axis=0)
    right_normal, right_spread = plain_norm(column_pairs)
    right_normed = (right_normal * gain_in + bias_in).astype(jnp.bfloat16)
    right_mask = (col_presence[:, None] * presence[None, :])[:, :, None]
    right_rows, right_lin, right_open = project(
        right_normed, proj_weights[2], proj_weights[3], right_mask
    )
    side_normal = take_cols(right_normal, first_key, tile_rows)
    side_spread = take_cols(right_spread, first_key, tile_rows)
    side_normed = take_cols(right_normed, first_key, tile_rows)
    side_lin = take_cols(right_lin, first_key, tile_rows)
    side_open = take_cols(right_open, first_key, tile_rows)
    mixing = jnp.einsum("ikh,jkh->ijh", left_rows, right_rows, preferred_element_type=jnp.float32)
    d_mixing, d_gate_in, grad_out, grad_gate, grad_gain, grad_bias = output_back(
        mixing, normed, cotangent, out_weights[0], out_weights[1], norm_gains[1], norm_biases[1]
    )
    portion = take_cols(right_rows, jnp.int32(0), lax.axis_size("col") * tile_cols)
    d_left = lax.psum_scatter(
        jnp.einsum("ijh,jkh->kih", d_mixing, portion, preferred_element_type=jnp.float32).astype(
            jnp.bfloat16
        ),
        "col",
        scatter_dimension=0,
        tiled=True,
    ).astype(jnp.float32)
    d_left = jnp.transpose(d_left, (1, 0, 2)).astype(jnp.bfloat16)
    portion = take_cols(left_rows, jnp.int32(0), lax.axis_size("row") * tile_rows)
    d_right = lax.psum_scatter(
        jnp.einsum("ijh,ikh->kjh", d_mixing, portion, preferred_element_type=jnp.float32).astype(
            jnp.bfloat16
        ),
        "row",
        scatter_dimension=0,
        tiled=True,
    ).astype(jnp.float32)
    d_right = jnp.transpose(d_right, (1, 0, 2)).astype(jnp.bfloat16)
    back_left, grad_lw, grad_lg = project_back(
        d_left, normed, left_lin, left_open, tile_mask, proj_weights[0], proj_weights[1]
    )
    back_right, grad_rw, grad_rg = project_back(
        d_right, side_normed, side_lin, side_open, side_mask, proj_weights[2], proj_weights[3]
    )
    main_back, gain_main, bias_main = norm_back(back_left + d_gate_in, normal, spread, gain_in)
    side_back, gain_side, bias_side = norm_back(back_right, side_normal, side_spread, gain_in)
    matrices = jnp.stack([grad_lw, grad_lg, grad_rw, grad_rg, grad_out, grad_gate])
    vectors = jnp.stack([gain_main + gain_side, bias_main + bias_side, grad_gain, grad_bias])
    matrices, vectors = lax.psum((matrices, vectors), ("row", "col"))
    grad_pair = main_back.astype(jnp.bfloat16)
    grad_pair_t = jnp.transpose(side_back, (1, 0, 2)).astype(jnp.bfloat16)
    return (grad_pair, grad_pair_t, matrices / tokens, vectors / tokens)


def dot_nt(first, second):
    return lax.dot_general(first, second, (((1,), (1,)), ((), ())), preferred_element_type=F32)


def dot_tn(first, second):
    return lax.dot_general(first, second, (((0,), (0,)), ((), ())), preferred_element_type=F32)


def dot_nn(first, second):
    return jnp.dot(first, second, preferred_element_type=F32)


def kernel(
    side,
    tile,
    tokens,
    mask_in,
    pair_in,
    cot_in,
    pw_in,
    ow_in,
    gain_in_ref,
    bias_in_ref,
    gp_ref,
    gpt_ref,
    gm_ref,
    gn_ref,
    mask_ref,
    pair_ref,
    cot_ref,
    pw_ref,
    ow_ref,
    gain_ref,
    bias_ref,
    lb,
    rb,
    pt,
    lf,
    rf,
    dmix,
    mix,
    normal_s,
    spread_s,
    normed_s,
    lin_s,
    open_s,
    gate_s,
    mask_s,
    tnormal_s,
    tspread_s,
    tnormed_s,
    tlin_s,
    topen_s,
    tmask_s,
    dgate_s,
    tback_s,
    sdl,
    sdr,
    rdl,
    rdr,
    grad,
    rowin,
    zpart,
    zin,
    whole,
    vec,
    rvec,
    zvec,
    cvec,
    in_sem,
    l_send,
    l_recv,
    r_send,
    r_recv,
    p_sem,
    dl_send,
    dl_recv,
    dr_send,
    dr_recv,
    rs_send,
    rs_recv,
    zs_send,
    zs_recv,
    za_send,
    za_recv,
    ra_send,
    ra_recv,
    vr_send,
    vr_recv,
    vz_send,
    vz_recv,
):
    r = lax.axis_index("row")
    c = lax.axis_index("col")
    cells = tile * tile
    rows = 256 // side
    part = rows // side

    def remote(src, dst, send, recv, row, col):
        return pltpu.make_async_remote_copy(
            src_ref=src,
            dst_ref=dst,
            send_sem=send,
            recv_sem=recv,
            device_id={"row": row, "col": col},
            device_id_type=MESH,
        )

    loads = [
        pltpu.make_async_copy(src, dst, in_sem.at[at_sem])
        for at_sem, (src, dst) in enumerate(
            (
                (pair_in, pair_ref),
                (pw_in, pw_ref),
                (mask_in, mask_ref),
                (gain_in_ref, gain_ref),
                (bias_in_ref, bias_ref),
                (ow_in, ow_ref),
                (cot_in, cot_ref),
            )
        )
    ]
    for load in loads:
        load.start()
    barrier = pltpu.get_barrier_semaphore()

    def greet(row, col):
        pl.semaphore_signal(
            barrier, inc=1, device_id={"row": row, "col": col}, device_id_type=MESH
        )

    for d in range(1, side):
        greet(lax.rem(r + d, side), c)
        greet(r, lax.rem(c + d, side))

    @pl.when(r != c)
    def _():
        greet(c, r)

    for load in loads:
        load.wait()
    gain_in = gain_ref[0:1, :]
    bias_in = bias_ref[0:1, :]
    gain_mix = gain_ref[1:2, :]
    bias_mix = bias_ref[1:2, :]

    sub = lax.broadcasted_iota(jnp.int32, (tile, 128), 0)
    row_vec = jnp.zeros((tile, 128), F32)
    col_vec = jnp.zeros((tile, 128), F32)
    row_bits = []
    col_bits = []
    for a in range(tile):
        row_bits.append(mask_ref[r * tile + a].astype(F32))
        col_bits.append(mask_ref[c * tile + a].astype(F32))
        row_vec = jnp.where(sub == a, row_bits[a], row_vec)
        col_vec = jnp.where(sub == a, col_bits[a], col_vec)
    for a in range(tile):
        mask_s[a * tile : (a + 1) * tile, :] = col_vec * row_bits[a]
        tmask_s[a * tile : (a + 1) * tile, :] = row_vec * col_bits[a]

    normal, spread = plain_norm(pair_ref[...].reshape(cells, 128))
    normed = (normal * gain_in + bias_in).astype(BF16)
    normal_s[...] = normal
    spread_s[...] = jnp.broadcast_to(spread, (cells, 128))
    normed_s[...] = normed
    pair_mask = mask_s[...]
    lin = dot_nn(normed, pw_ref[0])
    opened = jax.nn.sigmoid(dot_nn(normed, pw_ref[1]))
    lin_s[...] = lin
    open_s[...] = opened
    lb[c] = (opened * lin * pair_mask).astype(BF16).reshape(tile, tile, 128)

    @pl.when(r != c)
    def _():
        pl.semaphore_wait(barrier, 2 * side - 1)

    @pl.when(r == c)
    def _():
        pl.semaphore_wait(barrier, 2 * side - 2)

    def left_copy(d):
        return remote(
            lb.at[c], lb.at[c], l_send.at[d], l_recv.at[c], r, lax.rem(c + d, side)
        )

    def right_copy(d):
        return remote(
            rb.at[r], rb.at[r], r_send.at[d], r_recv.at[r], lax.rem(r + d, side), c
        )

    def pair_copy():
        return remote(pair_ref, pt, p_sem.at[0], p_sem.at[1], c, r)

    def left_arrival(b):
        return remote(lb.at[b], lb.at[b], l_send.at[0], l_recv.at[b], r, c)

    def right_arrival(b):
        return remote(rb.at[b], rb.at[b], r_send.at[0], r_recv.at[b], r, c)

    @pl.when(r != c)
    def _():
        pair_copy().start()

    for d in range(1, side):
        left_copy(d).start()

    @pl.when(r == c)
    def _():
        pt[...] = pair_ref[...]

    @pl.when(r != c)
    def _():
        pair_copy().wait_recv()

    tnormal, tspread = plain_norm(pt[...].reshape(cells, 128))
    tnormed = (tnormal * gain_in + bias_in).astype(BF16)
    tnormal_s[...] = tnormal
    tspread_s[...] = jnp.broadcast_to(tspread, (cells, 128))
    tnormed_s[...] = tnormed
    tlin = dot_nn(tnormed, pw_ref[2])
    topen = jax.nn.sigmoid(dot_nn(tnormed, pw_ref[3]))
    tlin_s[...] = tlin
    topen_s[...] = topen
    rb[r] = (topen * tlin * tmask_s[...]).astype(BF16).reshape(tile, tile, 128)
    for d in range(1, side):
        right_copy(d).start()

    gate_s[...] = jax.nn.sigmoid(dot_nn(normed, ow_ref[1]))

    def mix_block(d, accs):
        b = lax.rem(c + d, side)

        @pl.when(d > 0)
        def _():
            left_arrival(b).wait_recv()

        @pl.when(b != r)
        def _():
            right_arrival(b).wait_recv()

        base = pl.multiple_of(b * cells, cells)
        lf[pl.ds(base, cells), :] = lb[b].astype(F32).reshape(cells, 128)
        rf[pl.ds(base, cells), :] = rb[b].astype(F32).reshape(cells, 128)

        def step(k, accs):
            right = rf[pl.ds(base + k, tile, stride=tile), :]
            return tuple(
                accs[i] + lf[pl.ds(base + i * tile + k, 1), :] * right for i in range(tile)
            )

        return lax.fori_loop(0, tile, step, accs)

    zero = jnp.zeros((tile, 128), F32)
    accs = lax.fori_loop(0, side, mix_block, (zero,) * tile)
    for i in range(tile):
        mix[i * tile : (i + 1) * tile, :] = accs[i]

    xhat, mspread = plain_norm(mix[...])
    ynorm = (xhat * gain_mix + bias_mix).astype(BF16)
    upstream = cot_ref[...].reshape(cells, 128).astype(F32)
    gate = gate_s[...]
    d_out = (upstream * gate).astype(BF16)
    d_norm = dot_nt(d_out, ow_ref[0])
    scaled = d_norm * gain_mix
    d_mixing = mspread * (
        scaled
        - jnp.mean(scaled, axis=-1, keepdims=True)
        - xhat * jnp.mean(scaled * xhat, axis=-1, keepdims=True)
    )
    dmix[...] = d_mixing.astype(BF16).astype(F32)
    vec[...] = jnp.zeros_like(vec)
    vec[2:3, :] = jnp.sum(d_norm * xhat, axis=0, keepdims=True)
    vec[3:4, :] = jnp.sum(d_norm, axis=0, keepdims=True)
    sends = []

    def begin(copy):
        copy.start()
        sends.append(copy)

    def row_copy(src, dst, send, recv, base, x):
        return remote(src, dst, send.at[base + x], recv.at[base + r], x, c)

    def col_copy(src, dst, send, recv, base, y):
        return remote(src, dst, send.at[base + y], recv.at[base + c], r, y)

    def arrive(dst, recv, at_sem):
        remote(dst, dst, recv.at[at_sem], recv.at[at_sem], r, c).wait_recv()

    row_peers = [lax.rem(r + d, side) for d in range(1, side)]
    col_peers = [lax.rem(c + d, side) for d in range(1, side)]

    def chunk(t, size):
        return pl.ds(pl.multiple_of(t * size, size), size)

    def sum_of(ref, g):
        total = ref[g, 0].astype(F32)
        for x in range(1, side):
            total = total + ref[g, x].astype(F32)
        return total

    def scatter_row(g):
        for x in row_peers:
            begin(
                row_copy(
                    grad.at[g, chunk(x, rows)], rowin.at[g, r], rs_send, rs_recv, g * side, x
                )
            )
        rowin[g, r] = grad[g, chunk(r, rows), :]

    def scatter_col(g):
        for x in row_peers:
            arrive(rowin.at[g, x], rs_recv, g * side + x)
        zpart[g] = sum_of(rowin, g).astype(BF16)
        for y in col_peers:
            begin(
                col_copy(
                    zpart.at[g, chunk(y, part)], zin.at[g, c], zs_send, zs_recv, g * side, y
                )
            )
        zin[g, c] = zpart[g, chunk(c, part), :]

    def gather_col(g):
        for y in col_peers:
            arrive(zin.at[g, y], zs_recv, g * side + y)
        whole[g, r, c] = (sum_of(zin, g) / tokens).astype(BF16)
        for y in col_peers:
            begin(
                col_copy(
                    whole.at[g, r, c], whole.at[g, r, c], za_send, za_recv, g * side, y
                )
            )

    def gather_row(g):
        for y in col_peers:
            arrive(whole.at[g, r, y], za_recv, g * side + y)
        for x in row_peers:
            begin(
                row_copy(whole.at[g, r], whole.at[g, r], ra_send, ra_recv, g * side, x)
            )

    def finish(g, first):
        for x in row_peers:
            arrive(whole.at[g, x], ra_recv, g * side + x)
        gm_ref[first : first + 2] = whole[g].astype(F32).reshape(2, 128, 128)

    group = 4

    def left_part(b, out, slot):
        def step(g, carry):
            first = g * group
            sums = [zero] * group
            for j in range(tile):
                right = rf[pl.ds(pl.multiple_of(b * cells + j * tile, tile), tile), :]
                for q in range(group):
                    sums[q] = sums[q] + dmix[pl.ds((first + q) * tile + j, 1), :] * right
            for q in range(group):
                out[slot, first + q] = sums[q].astype(BF16)
            return carry

        lax.fori_loop(0, tile // group, step, 0)

    def right_part(b, out, slot):
        def step(g, carry):
            first = g * group
            sums = [zero] * group
            for i in range(tile):
                left = lf[pl.ds(pl.multiple_of(b * cells + i * tile, tile), tile), :]
                for q in range(group):
                    sums[q] = sums[q] + dmix[pl.ds(i * tile + first + q, 1), :] * left
            for q in range(group):
                out[slot, first + q] = sums[q].astype(BF16)
            return carry

        lax.fori_loop(0, tile // group, step, 0)

    def dl_copy(b):
        return remote(sdl.at[b], rdl.at[c], dl_send.at[b], dl_recv.at[c], r, b)

    def dr_copy(b):
        return remote(sdr.at[b], rdr.at[r], dr_send.at[b], dr_recv.at[r], b, c)

    def dl_arrival(b):
        return remote(sdl.at[b], rdl.at[b], dl_send.at[b], dl_recv.at[b], r, c)

    def dr_arrival(b):
        return remote(sdr.at[b], rdr.at[b], dr_send.at[b], dr_recv.at[b], r, c)

    def part_step(d, carry):
        b = lax.rem(c + d, side)
        left_part(b, sdl, b)
        dl_copy(b).start()
        b = lax.rem(r + d, side)
        right_part(b, sdr, b)
        dr_copy(b).start()
        return carry

    lax.fori_loop(1, side, part_step, 0)
    outer = dot_nn(ynorm, ow_ref[0])
    d_open = (upstream * outer * gate * (1.0 - gate)).astype(BF16)
    grad[0, 0:128, :] = dot_tn(ynorm, d_out).astype(BF16)
    grad[0, 128:256, :] = dot_tn(normed_s[...], d_open).astype(BF16)
    dgate_s[...] = dot_nt(d_open, ow_ref[1])

    scatter_row(0)
    left_part(c, rdl, c)
    right_part(r, rdr, r)

    def branch_back(received, mask, opened, linear, normed, first, g):
        total = received[0].astype(F32)
        for s in range(1, side):
            total = total + received[s].astype(F32)
        up = total.astype(BF16).astype(F32).reshape(cells, 128) * mask
        d_lin = (up * opened).astype(BF16)
        d_gate = (up * linear * opened * (1.0 - opened)).astype(BF16)
        grad[g, 0:128, :] = dot_tn(normed, d_lin).astype(BF16)
        grad[g, 128:256, :] = dot_tn(normed, d_gate).astype(BF16)
        return dot_nt(d_lin, pw_ref[first]) + dot_nt(d_gate, pw_ref[first + 1])

    for d in range(1, side):
        dr_arrival(lax.rem(r + d, side)).wait_recv()
    back_right = branch_back(rdr, tmask_s[...], topen_s[...], tlin_s[...], tnormed_s[...], 2, 1)
    scatter_row(1)
    scatter_col(0)
    for d in range(1, side):
        dl_arrival(lax.rem(c + d, side)).wait_recv()
    back_left = branch_back(rdl, mask_s[...], open_s[...], lin_s[...], normed_s[...], 0, 2)
    scatter_row(2)
    scatter_col(1)
    gather_col(0)

    main, gain_main, bias_main = norm_back(
        back_left + dgate_s[...], normal_s[...], spread_s[...], gain_in
    )
    turned, gain_side, bias_side = norm_back(
        back_right, tnormal_s[...], tspread_s[...], gain_in
    )
    vec[0:1, :] = (gain_main + gain_side)[None, :]
    vec[1:2, :] = (bias_main + bias_side)[None, :]
    for x in row_peers:
        begin(row_copy(vec, rvec.at[0, r], vr_send, vr_recv, 0, x))
    rvec[0, r] = vec[...]

    scatter_col(2)
    gather_col(1)
    gather_row(0)
    gp_ref[...] = main.astype(BF16).reshape(tile, tile, 128)
    tback_s[...] = turned
    for k in range(tile):
        gpt_ref[k] = tback_s[pl.ds(k, tile, stride=tile), :].astype(BF16)

    for x in row_peers:
        arrive(rvec.at[0, x], vr_recv, x)
    zvec[...] = sum_of(rvec, 0)
    for y in col_peers:
        begin(col_copy(zvec, cvec.at[0, c], vz_send, vz_recv, 0, y))
    cvec[0, c] = zvec[...]

    gather_col(2)
    gather_row(1)
    gather_row(2)
    for y in col_peers:
        arrive(cvec.at[0, y], vz_recv, y)
    gn_ref[...] = sum_of(cvec, 0)[0:4, :] / tokens

    for d in range(1, side):
        left_copy(d).wait_send()
        right_copy(d).wait_send()
        dl_copy(lax.rem(c + d, side)).wait_send()
        dr_copy(lax.rem(r + d, side)).wait_send()

    @pl.when(r != c)
    def _():
        pair_copy().wait_send()

    finish(0, 4)
    finish(1, 2)
    finish(2, 0)
    for copy in sends:
        copy.wait_send()


def hand_over(*refs):
    sems = refs[8]
    copies = [pltpu.make_async_copy(refs[x], refs[x + 4], sems.at[x]) for x in range(4)]
    for copy in copies:
        copy.start()
    for copy in copies:
        copy.wait()


def fused(side, pair, cotangent, token_mask, proj_weights, out_weights, norm_gains, norm_biases):
    tile = pair.shape[0]
    tokens = token_mask.shape[0]
    cells = tile * tile
    rows = 256 // side
    part = rows // side
    block = (side, tile, tile, 128)
    wide = pltpu.VMEM((cells, 128), F32)
    slim = pltpu.VMEM((cells, 128), BF16)
    dma = pltpu.SemaphoreType.DMA
    vmem = pl.BlockSpec(memory_space=pltpu.VMEM)
    results = pl.pallas_call(
        functools.partial(kernel, side, tile, tokens),
        out_shape=(
            jax.ShapeDtypeStruct((tile, tile, 128), BF16),
            jax.ShapeDtypeStruct((tile, tile, 128), BF16),
            jax.ShapeDtypeStruct((6, 128, 128), F32),
            jax.ShapeDtypeStruct((4, 128), F32),
        ),
        in_specs=[pl.BlockSpec(memory_space=pltpu.HBM)] * 7,
        out_specs=(vmem,) * 4,
        scratch_shapes=[
            pltpu.SMEM(token_mask.shape, jnp.int32),
            pltpu.VMEM(pair.shape, BF16),
            pltpu.VMEM(pair.shape, BF16),
            pltpu.VMEM(proj_weights.shape, BF16),
            pltpu.VMEM(out_weights.shape, BF16),
            pltpu.VMEM(norm_gains.shape, F32),
            pltpu.VMEM(norm_biases.shape, F32),
            pltpu.VMEM(block, BF16),
            pltpu.VMEM(block, BF16),
            pltpu.VMEM((tile, tile, 128), BF16),
            pltpu.VMEM((side * cells, 128), F32),
            pltpu.VMEM((side * cells, 128), F32),
            wide,
            wide,
            wide,
            wide,
            slim,
            wide,
            wide,
            wide,
            wide,
            wide,
            wide,
            slim,
            wide,
            wide,
            wide,
            wide,
            wide,
            pltpu.VMEM(block, BF16),
            pltpu.VMEM(block, BF16),
            pltpu.VMEM(block, BF16),
            pltpu.VMEM(block, BF16),
            pltpu.VMEM((3, 256, 128), BF16),
            pltpu.VMEM((3, side, rows, 128), BF16),
            pltpu.VMEM((3, rows, 128), BF16),
            pltpu.VMEM((3, side, part, 128), BF16),
            pltpu.VMEM((3, side, side, part, 128), BF16),
            pltpu.VMEM((8, 128), F32),
            pltpu.VMEM((1, side, 8, 128), F32),
            pltpu.VMEM((8, 128), F32),
            pltpu.VMEM((1, side, 8, 128), F32),
            dma((7,)),
            dma((side,)),
            dma((side,)),
            dma((side,)),
            dma((side,)),
            dma((2,)),
            dma((side,)),
            dma((side,)),
            dma((side,)),
            dma((side,)),
        ]
        + [dma((3 * side,))] * 8
        + [dma((side,))] * 4,
        compiler_params=pltpu.CompilerParams(
            collective_id=0, has_side_effects=True, vmem_limit_bytes=63 * 1024 * 1024
        ),
    )(token_mask, pair, cotangent, proj_weights, out_weights, norm_gains, norm_biases)
    main = pl.BlockSpec(memory_space=pltpu.HBM)
    return pl.pallas_call(
        hand_over,
        out_shape=tuple(jax.ShapeDtypeStruct(x.shape, x.dtype) for x in results),
        in_specs=[vmem] * 4,
        out_specs=(main,) * 4,
        scratch_shapes=[dma((4,))],
    )(*results)


def device_program(*args):
    rows, cols = lax.axis_size("row"), lax.axis_size("col")
    pair = args[0]
    square = rows == cols and pair.shape[0] == pair.shape[1] == 16
    if square and 256 % (16 * rows * cols) == 0 and pair.shape[2] == 128:
        return fused(rows, *args)
    return per_device(*args)


def solution(mesh):
    in_specs = (
        P(("grp", "row"), "col", None),
        P(("grp", "row"), "col", None),
        P("grp"),
        P(),
        P(),
        P(),
        P(),
    )
    out_specs = (
        P(("grp", "row"), "col", None),
        P(("grp", "row"), "col", None),
        P("grp", None, None),
        P("grp", None),
    )
    return jax.shard_map(
        device_program, mesh=mesh, in_specs=in_specs, out_specs=out_specs, check_vma=False
    )
```

```python
import functools

import jax
import jax.numpy as jnp
from jax import lax
from jax.experimental import pallas as pl
from jax.experimental.pallas import tpu as pltpu
from jax.sharding import PartitionSpec as P

MESH = pl.DeviceIdType.MESH
F32 = jnp.float32
BF16 = jnp.bfloat16

EPS = 1e-05


def spread_2(x, axis, root):
    mine = lax.axis_index(axis) == root
    return lax.psum(jnp.where(mine, x, jnp.zeros_like(x)), axis)


def plain_norm(source):
    source = source.astype(jnp.float32)
    center = source - jnp.mean(source, axis=-1, keepdims=True)
    spread = lax.rsqrt(jnp.mean(center * center, axis=-1, keepdims=True) + EPS)
    return (center * spread, spread)


def matmul(operand, weight):
    extent = operand.shape
    flattened = operand.reshape(-1, extent[-1])
    result = jnp.dot(flattened, weight, preferred_element_type=jnp.float32)
    return result.reshape(extent[:-1] + (weight.shape[-1],))


def column_sum(values):
    return jnp.sum(values.reshape(-1, values.shape[-1]), axis=0)


def outer_sum(first, second):
    return jnp.dot(
        first.reshape(-1, first.shape[-1]).T,
        second.reshape(-1, second.shape[-1]),
        preferred_element_type=jnp.float32,
    )


def project(normed, weight, gate_weight, pair_mask):
    linear = matmul(normed, weight)
    opened = jax.nn.sigmoid(matmul(normed, gate_weight))
    return ((opened * linear * pair_mask).astype(jnp.bfloat16), linear, opened)


def project_back(d_proj, normed, linear, opened, pair_mask, weight, gate_weight):
    upstream = d_proj.astype(jnp.float32) * pair_mask
    d_linear = (upstream * opened).astype(jnp.bfloat16)
    d_opened = (upstream * linear * opened * (1.0 - opened)).astype(jnp.bfloat16)
    grad_weight = outer_sum(normed, d_linear)
    grad_gate = outer_sum(normed, d_opened)
    returned = matmul(d_linear, weight.T) + matmul(d_opened, gate_weight.T)
    return (returned, grad_weight, grad_gate)


def norm_back(upstream, normal, spread, gain_vec):
    scaled_up = upstream * gain_vec
    returned = spread * (
        scaled_up
        - jnp.mean(scaled_up, axis=-1, keepdims=True)
        - normal * jnp.mean(scaled_up * normal, axis=-1, keepdims=True)
    )
    return (returned, column_sum(upstream * normal), column_sum(upstream))


def output_back(mixing, normed, cotangent, out_weight, gate_weight, gain_vec, bias_vec):
    normal, spread = plain_norm(mixing)
    ynorm = (normal * gain_vec + bias_vec).astype(jnp.bfloat16)
    outer = matmul(ynorm, out_weight)
    opened = jax.nn.sigmoid(matmul(normed, gate_weight))
    upstream = cotangent.astype(jnp.float32)
    d_out = (upstream * opened).astype(jnp.bfloat16)
    d_opened = (upstream * outer * opened * (1.0 - opened)).astype(jnp.bfloat16)
    grad_out = outer_sum(ynorm, d_out)
    grad_gate = outer_sum(normed, d_opened)
    d_norm = matmul(d_out, out_weight.T)
    d_mixing, grad_gain, grad_bias = norm_back(d_norm, normal, spread, gain_vec)
    return (
        d_mixing.astype(jnp.bfloat16),
        matmul(d_opened, gate_weight.T),
        grad_out,
        grad_gate,
        grad_gain,
        grad_bias,
    )


def take_cols(values, offset, amount):
    return lax.dynamic_slice_in_dim(values, offset, amount, 1)


def per_device(pair, cotangent, token_mask, proj_weights, out_weights, norm_gains, norm_biases):
    tile_rows = pair.shape[0]
    tile_cols = pair.shape[1]
    tokens = token_mask.shape[0]
    repeat_count = lax.axis_size("row") // lax.axis_size("col")
    row_index = lax.axis_index("row")
    col_index = lax.axis_index("col")
    presence = token_mask.astype(jnp.float32)
    row_presence = lax.dynamic_slice_in_dim(presence, row_index * tile_rows, tile_rows)
    col_presence = lax.dynamic_slice_in_dim(presence, col_index * tile_cols, tile_cols)
    tile_mask = (row_presence[:, None] * col_presence[None, :])[:, :, None]
    gain_in = norm_gains[0]
    bias_in = norm_biases[0]
    strip = lax.all_gather(pair, "col", axis=1, tiled=True)
    strip_normal, strip_spread = plain_norm(strip)
    strip_normed = (strip_normal * gain_in + bias_in).astype(jnp.bfloat16)
    strip_mask = (row_presence[:, None] * presence[None, :])[:, :, None]
    left_rows, strip_lin, strip_open = project(
        strip_normed, proj_weights[0], proj_weights[1], strip_mask
    )
    first_col = col_index * tile_cols
    normal = take_cols(strip_normal, first_col, tile_cols)
    spread = take_cols(strip_spread, first_col, tile_cols)
    normed = take_cols(strip_normed, first_col, tile_cols)
    left_lin = take_cols(strip_lin, first_col, tile_cols)
    left_open = take_cols(strip_open, first_col, tile_cols)
    first_key = row_index * tile_rows
    side_mask = (col_presence[:, None] * row_presence[None, :])[:, :, None]
    pieces = []
    for offset in range(repeat_count):
        pieces.append(spread_2(strip, "row", col_index * repeat_count + offset))
    column_pairs = jnp.concatenate(pieces, axis=0)
    right_normal, right_spread = plain_norm(column_pairs)
    right_normed = (right_normal * gain_in + bias_in).astype(jnp.bfloat16)
    right_mask = (col_presence[:, None] * presence[None, :])[:, :, None]
    right_rows, right_lin, right_open = project(
        right_normed, proj_weights[2], proj_weights[3], right_mask
    )
    side_normal = take_cols(right_normal, first_key, tile_rows)
    side_spread = take_cols(right_spread, first_key, tile_rows)
    side_normed = take_cols(right_normed, first_key, tile_rows)
    side_lin = take_cols(right_lin, first_key, tile_rows)
    side_open = take_cols(right_open, first_key, tile_rows)
    mixing = jnp.einsum("ikh,jkh->ijh", left_rows, right_rows, preferred_element_type=jnp.float32)
    d_mixing, d_gate_in, grad_out, grad_gate, grad_gain, grad_bias = output_back(
        mixing, normed, cotangent, out_weights[0], out_weights[1], norm_gains[1], norm_biases[1]
    )
    portion = take_cols(right_rows, jnp.int32(0), lax.axis_size("col") * tile_cols)
    d_left = lax.psum_scatter(
        jnp.einsum("ijh,jkh->kih", d_mixing, portion, preferred_element_type=jnp.float32).astype(
            jnp.bfloat16
        ),
        "col",
        scatter_dimension=0,
        tiled=True,
    ).astype(jnp.float32)
    d_left = jnp.transpose(d_left, (1, 0, 2)).astype(jnp.bfloat16)
    portion = take_cols(left_rows, jnp.int32(0), lax.axis_size("row") * tile_rows)
    d_right = lax.psum_scatter(
        jnp.einsum("ijh,ikh->kjh", d_mixing, portion, preferred_element_type=jnp.float32).astype(
            jnp.bfloat16
        ),
        "row",
        scatter_dimension=0,
        tiled=True,
    ).astype(jnp.float32)
    d_right = jnp.transpose(d_right, (1, 0, 2)).astype(jnp.bfloat16)
    back_left, grad_lw, grad_lg = project_back(
        d_left, normed, left_lin, left_open, tile_mask, proj_weights[0], proj_weights[1]
    )
    back_right, grad_rw, grad_rg = project_back(
        d_right, side_normed, side_lin, side_open, side_mask, proj_weights[2], proj_weights[3]
    )
    main_back, gain_main, bias_main = norm_back(back_left + d_gate_in, normal, spread, gain_in)
    side_back, gain_side, bias_side = norm_back(back_right, side_normal, side_spread, gain_in)
    matrices = jnp.stack([grad_lw, grad_lg, grad_rw, grad_rg, grad_out, grad_gate])
    vectors = jnp.stack([gain_main + gain_side, bias_main + bias_side, grad_gain, grad_bias])
    matrices, vectors = lax.psum((matrices, vectors), ("row", "col"))
    grad_pair = main_back.astype(jnp.bfloat16)
    grad_pair_t = jnp.transpose(side_back, (1, 0, 2)).astype(jnp.bfloat16)
    return (grad_pair, grad_pair_t, matrices / tokens, vectors / tokens)


def dot_nt(first, second):
    return lax.dot_general(first, second, (((1,), (1,)), ((), ())), preferred_element_type=F32)


def dot_tn(first, second):
    return lax.dot_general(first, second, (((0,), (0,)), ((), ())), preferred_element_type=F32)


def dot_nn(first, second):
    return jnp.dot(first, second, preferred_element_type=F32)


def kernel(
    side,
    tile,
    tokens,
    mask_in,
    pair_in,
    cot_in,
    pw_in,
    ow_in,
    gain_in_ref,
    bias_in_ref,
    gp_ref,
    gpt_ref,
    gm_ref,
    gn_ref,
    mask_ref,
    pair_ref,
    cot_ref,
    pw_ref,
    ow_ref,
    gain_ref,
    bias_ref,
    lb,
    rb,
    pt,
    lf,
    rf,
    dmix,
    mix,
    normal_s,
    spread_s,
    normed_s,
    lin_s,
    open_s,
    gate_s,
    mask_s,
    tnormal_s,
    tspread_s,
    tnormed_s,
    tlin_s,
    topen_s,
    tmask_s,
    dgate_s,
    tback_s,
    sdl,
    sdr,
    rdl,
    rdr,
    grad,
    rowin,
    zpart,
    zin,
    whole,
    vec,
    rvec,
    zvec,
    cvec,
    in_sem,
    l_send,
    l_recv,
    r_send,
    r_recv,
    p_sem,
    dl_send,
    dl_recv,
    dr_send,
    dr_recv,
    rs_send,
    rs_recv,
    zs_send,
    zs_recv,
    ra_send,
    ra_recv,
    vr_send,
    vr_recv,
    vz_send,
    vz_recv,
):
    r = lax.axis_index("row")
    c = lax.axis_index("col")
    cells = tile * tile
    rows = 256 // side

    def remote(src, dst, send, recv, row, col):
        return pltpu.make_async_remote_copy(
            src_ref=src,
            dst_ref=dst,
            send_sem=send,
            recv_sem=recv,
            device_id={"row": row, "col": col},
            device_id_type=MESH,
        )

    loads = [
        pltpu.make_async_copy(src, dst, in_sem.at[at_sem])
        for at_sem, (src, dst) in enumerate(
            (
                (pair_in, pair_ref),
                (pw_in, pw_ref),
                (mask_in, mask_ref),
                (gain_in_ref, gain_ref),
                (bias_in_ref, bias_ref),
                (ow_in, ow_ref),
                (cot_in, cot_ref),
            )
        )
    ]
    for load in loads:
        load.start()
    barrier = pltpu.get_barrier_semaphore()

    def greet(row, col):
        pl.semaphore_signal(
            barrier, inc=1, device_id={"row": row, "col": col}, device_id_type=MESH
        )

    for d in range(1, side):
        greet(lax.rem(r + d, side), c)
        greet(r, lax.rem(c + d, side))

    @pl.when(r != c)
    def _():
        greet(c, r)

    for load in loads:
        load.wait()
    gain_in = gain_ref[0:1, :]
    bias_in = bias_ref[0:1, :]
    gain_mix = gain_ref[1:2, :]
    bias_mix = bias_ref[1:2, :]

    sub = lax.broadcasted_iota(jnp.int32, (tile, 128), 0)
    row_vec = jnp.zeros((tile, 128), F32)
    col_vec = jnp.zeros((tile, 128), F32)
    row_bits = []
    col_bits = []
    for a in range(tile):
        row_bits.append(mask_ref[r * tile + a].astype(F32))
        col_bits.append(mask_ref[c * tile + a].astype(F32))
        row_vec = jnp.where(sub == a, row_bits[a], row_vec)
        col_vec = jnp.where(sub == a, col_bits[a], col_vec)
    for a in range(tile):
        mask_s[a * tile : (a + 1) * tile, :] = col_vec * row_bits[a]
        tmask_s[a * tile : (a + 1) * tile, :] = row_vec * col_bits[a]

    normal, spread = plain_norm(pair_ref[...].reshape(cells, 128))
    normed = (normal * gain_in + bias_in).astype(BF16)
    normal_s[...] = normal
    spread_s[...] = jnp.broadcast_to(spread, (cells, 128))
    normed_s[...] = normed
    pair_mask = mask_s[...]
    lin = dot_nn(normed, pw_ref[0])
    opened = jax.nn.sigmoid(dot_nn(normed, pw_ref[1]))
    lin_s[...] = lin
    open_s[...] = opened
    lb[c] = (opened * lin * pair_mask).astype(BF16).reshape(tile, tile, 128)

    @pl.when(r != c)
    def _():
        pl.semaphore_wait(barrier, 2 * side - 1)

    @pl.when(r == c)
    def _():
        pl.semaphore_wait(barrier, 2 * side - 2)

    def left_copy(d):
        return remote(
            lb.at[c], lb.at[c], l_send.at[d], l_recv.at[c], r, lax.rem(c + d, side)
        )

    def right_copy(d):
        return remote(
            rb.at[r], rb.at[r], r_send.at[d], r_recv.at[r], lax.rem(r + d, side), c
        )

    def pair_copy():
        return remote(pair_ref, pt, p_sem.at[0], p_sem.at[1], c, r)

    def left_arrival(b):
        return remote(lb.at[b], lb.at[b], l_send.at[0], l_recv.at[b], r, c)

    def right_arrival(b):
        return remote(rb.at[b], rb.at[b], r_send.at[0], r_recv.at[b], r, c)

    @pl.when(r != c)
    def _():
        pair_copy().start()

    for d in range(1, side):
        left_copy(d).start()

    @pl.when(r == c)
    def _():
        pt[...] = pair_ref[...]

    @pl.when(r != c)
    def _():
        pair_copy().wait_recv()

    tnormal, tspread = plain_norm(pt[...].reshape(cells, 128))
    tnormed = (tnormal * gain_in + bias_in).astype(BF16)
    tnormal_s[...] = tnormal
    tspread_s[...] = jnp.broadcast_to(tspread, (cells, 128))
    tnormed_s[...] = tnormed
    tlin = dot_nn(tnormed, pw_ref[2])
    topen = jax.nn.sigmoid(dot_nn(tnormed, pw_ref[3]))
    tlin_s[...] = tlin
    topen_s[...] = topen
    rb[r] = (topen * tlin * tmask_s[...]).astype(BF16).reshape(tile, tile, 128)
    for d in range(1, side):
        right_copy(d).start()

    gate_s[...] = jax.nn.sigmoid(dot_nn(normed, ow_ref[1]))

    def mix_block(d, accs):
        b = lax.rem(c + d, side)

        @pl.when(d > 0)
        def _():
            left_arrival(b).wait_recv()

        @pl.when(b != r)
        def _():
            right_arrival(b).wait_recv()

        base = pl.multiple_of(b * cells, cells)
        lf[pl.ds(base, cells), :] = lb[b].astype(F32).reshape(cells, 128)
        rf[pl.ds(base, cells), :] = rb[b].astype(F32).reshape(cells, 128)

        def step(k, accs):
            right = rf[pl.ds(base + k, tile, stride=tile), :]
            return tuple(
                accs[i] + lf[pl.ds(base + i * tile + k, 1), :] * right for i in range(tile)
            )

        return lax.fori_loop(0, tile, step, accs)

    zero = jnp.zeros((tile, 128), F32)
    accs = lax.fori_loop(0, side, mix_block, (zero,) * tile)
    for i in range(tile):
        mix[i * tile : (i + 1) * tile, :] = accs[i]

    xhat, mspread = plain_norm(mix[...])
    ynorm = (xhat * gain_mix + bias_mix).astype(BF16)
    upstream = cot_ref[...].reshape(cells, 128).astype(F32)
    gate = gate_s[...]
    d_out = (upstream * gate).astype(BF16)
    d_norm = dot_nt(d_out, ow_ref[0])
    scaled = d_norm * gain_mix
    d_mixing = mspread * (
        scaled
        - jnp.mean(scaled, axis=-1, keepdims=True)
        - xhat * jnp.mean(scaled * xhat, axis=-1, keepdims=True)
    )
    dmix[...] = d_mixing.astype(BF16).astype(F32)
    vec[...] = jnp.zeros_like(vec)
    vec[2:3, :] = jnp.sum(d_norm * xhat, axis=0, keepdims=True)
    vec[3:4, :] = jnp.sum(d_norm, axis=0, keepdims=True)
    sends = []

    def begin(copy):
        copy.start()
        sends.append(copy)

    def row_copy(src, dst, send, recv, base, x):
        return remote(src, dst, send.at[base + x], recv.at[base + r], x, c)

    def col_copy(src, dst, send, recv, base, y):
        return remote(src, dst, send.at[base + y], recv.at[base + c], r, y)

    def arrive(dst, recv, at_sem):
        remote(dst, dst, recv.at[at_sem], recv.at[at_sem], r, c).wait_recv()

    row_peers = [lax.rem(r + d, side) for d in range(1, side)]
    col_peers = [lax.rem(c + d, side) for d in range(1, side)]

    def chunk(t, size):
        return pl.ds(pl.multiple_of(t * size, size), size)

    def sum_of(ref, g):
        total = ref[g, 0].astype(F32)
        for x in range(1, side):
            total = total + ref[g, x].astype(F32)
        return total

    def scatter_row(g):
        for x in row_peers:
            begin(
                row_copy(
                    grad.at[g, chunk(x, rows)], rowin.at[g, r], rs_send, rs_recv, g * side, x
                )
            )
        rowin[g, r] = grad[g, chunk(r, rows), :]

    def scatter_col(g):
        for x in row_peers:
            arrive(rowin.at[g, x], rs_recv, g * side + x)
        zpart[g] = sum_of(rowin, g).astype(BF16)
        for y in col_peers:
            begin(col_copy(zpart.at[g], zin.at[g, c], zs_send, zs_recv, g * side, y))
        zin[g, c] = zpart[g]

    def gather_col(g):
        for y in col_peers:
            arrive(zin.at[g, y], zs_recv, g * side + y)
        whole[g, r] = (sum_of(zin, g) / tokens).astype(BF16)

    def gather_row(g):
        for x in row_peers:
            begin(
                row_copy(whole.at[g, r], whole.at[g, r], ra_send, ra_recv, g * side, x)
            )

    def finish(g, first):
        for x in row_peers:
            arrive(whole.at[g, x], ra_recv, g * side + x)
        gm_ref[first : first + 2] = whole[g].astype(F32).reshape(2, 128, 128)

    group = 4

    def left_part(b, out, slot):
        def step(g, carry):
            first = g * group
            sums = [zero] * group
            for j in range(tile):
                right = rf[pl.ds(pl.multiple_of(b * cells + j * tile, tile), tile), :]
                for q in range(group):
                    sums[q] = sums[q] + dmix[pl.ds((first + q) * tile + j, 1), :] * right
            for q in range(group):
                out[slot, first + q] = sums[q].astype(BF16)
            return carry

        lax.fori_loop(0, tile // group, step, 0)

    def right_part(b, out, slot):
        def step(g, carry):
            first = g * group
            sums = [zero] * group
            for i in range(tile):
                left = lf[pl.ds(pl.multiple_of(b * cells + i * tile, tile), tile), :]
                for q in range(group):
                    sums[q] = sums[q] + dmix[pl.ds(i * tile + first + q, 1), :] * left
            for q in range(group):
                out[slot, first + q] = sums[q].astype(BF16)
            return carry

        lax.fori_loop(0, tile // group, step, 0)

    def dl_copy(b):
        return remote(sdl.at[b], rdl.at[c], dl_send.at[b], dl_recv.at[c], r, b)

    def dr_copy(b):
        return remote(sdr.at[b], rdr.at[r], dr_send.at[b], dr_recv.at[r], b, c)

    def dl_arrival(b):
        return remote(sdl.at[b], rdl.at[b], dl_send.at[b], dl_recv.at[b], r, c)

    def dr_arrival(b):
        return remote(sdr.at[b], rdr.at[b], dr_send.at[b], dr_recv.at[b], r, c)

    def part_step(d, carry):
        b = lax.rem(c + d, side)
        left_part(b, sdl, b)
        dl_copy(b).start()
        b = lax.rem(r + d, side)
        right_part(b, sdr, b)
        dr_copy(b).start()
        return carry

    lax.fori_loop(1, side, part_step, 0)
    outer = dot_nn(ynorm, ow_ref[0])
    d_open = (upstream * outer * gate * (1.0 - gate)).astype(BF16)
    grad[0, 0:128, :] = dot_tn(ynorm, d_out).astype(BF16)
    grad[0, 128:256, :] = dot_tn(normed_s[...], d_open).astype(BF16)
    dgate_s[...] = dot_nt(d_open, ow_ref[1])

    scatter_row(0)
    left_part(c, rdl, c)
    right_part(r, rdr, r)

    def branch_back(received, mask, opened, linear, normed, first, g):
        total = received[0].astype(F32)
        for s in range(1, side):
            total = total + received[s].astype(F32)
        up = total.astype(BF16).astype(F32).reshape(cells, 128) * mask
        d_lin = (up * opened).astype(BF16)
        d_gate = (up * linear * opened * (1.0 - opened)).astype(BF16)
        grad[g, 0:128, :] = dot_tn(normed, d_lin).astype(BF16)
        grad[g, 128:256, :] = dot_tn(normed, d_gate).astype(BF16)
        return dot_nt(d_lin, pw_ref[first]) + dot_nt(d_gate, pw_ref[first + 1])

    for d in range(1, side):
        dr_arrival(lax.rem(r + d, side)).wait_recv()
    back_right = branch_back(rdr, tmask_s[...], topen_s[...], tlin_s[...], tnormed_s[...], 2, 1)
    scatter_row(1)
    scatter_col(0)
    for d in range(1, side):
        dl_arrival(lax.rem(c + d, side)).wait_recv()
    back_left = branch_back(rdl, mask_s[...], open_s[...], lin_s[...], normed_s[...], 0, 2)
    scatter_row(2)
    scatter_col(1)
    gather_col(0)
    gather_row(0)

    main, gain_main, bias_main = norm_back(
        back_left + dgate_s[...], normal_s[...], spread_s[...], gain_in
    )
    turned, gain_side, bias_side = norm_back(
        back_right, tnormal_s[...], tspread_s[...], gain_in
    )
    vec[0:1, :] = (gain_main + gain_side)[None, :]
    vec[1:2, :] = (bias_main + bias_side)[None, :]
    for x in row_peers:
        begin(row_copy(vec, rvec.at[0, r], vr_send, vr_recv, 0, x))
    rvec[0, r] = vec[...]

    scatter_col(2)
    gather_col(1)
    gather_row(1)
    gp_ref[...] = main.astype(BF16).reshape(tile, tile, 128)
    tback_s[...] = turned
    for k in range(tile):
        gpt_ref[k] = tback_s[pl.ds(k, tile, stride=tile), :].astype(BF16)

    for x in row_peers:
        arrive(rvec.at[0, x], vr_recv, x)
    zvec[...] = sum_of(rvec, 0)
    for y in col_peers:
        begin(col_copy(zvec, cvec.at[0, c], vz_send, vz_recv, 0, y))
    cvec[0, c] = zvec[...]

    gather_col(2)
    gather_row(2)
    for y in col_peers:
        arrive(cvec.at[0, y], vz_recv, y)
    gn_ref[...] = sum_of(cvec, 0)[0:4, :] / tokens

    for d in range(1, side):
        left_copy(d).wait_send()
        right_copy(d).wait_send()
        dl_copy(lax.rem(c + d, side)).wait_send()
        dr_copy(lax.rem(r + d, side)).wait_send()

    @pl.when(r != c)
    def _():
        pair_copy().wait_send()

    finish(0, 4)
    finish(1, 2)
    finish(2, 0)
    for copy in sends:
        copy.wait_send()


def hand_over(*refs):
    sems = refs[8]
    copies = [pltpu.make_async_copy(refs[x], refs[x + 4], sems.at[x]) for x in range(4)]
    for copy in copies:
        copy.start()
    for copy in copies:
        copy.wait()


def fused(side, pair, cotangent, token_mask, proj_weights, out_weights, norm_gains, norm_biases):
    tile = pair.shape[0]
    tokens = token_mask.shape[0]
    cells = tile * tile
    rows = 256 // side
    block = (side, tile, tile, 128)
    wide = pltpu.VMEM((cells, 128), F32)
    slim = pltpu.VMEM((cells, 128), BF16)
    dma = pltpu.SemaphoreType.DMA
    vmem = pl.BlockSpec(memory_space=pltpu.VMEM)
    results = pl.pallas_call(
        functools.partial(kernel, side, tile, tokens),
        out_shape=(
            jax.ShapeDtypeStruct((tile, tile, 128), BF16),
            jax.ShapeDtypeStruct((tile, tile, 128), BF16),
            jax.ShapeDtypeStruct((6, 128, 128), F32),
            jax.ShapeDtypeStruct((4, 128), F32),
        ),
        in_specs=[pl.BlockSpec(memory_space=pltpu.HBM)] * 7,
        out_specs=(vmem,) * 4,
        scratch_shapes=[
            pltpu.SMEM(token_mask.shape, jnp.int32),
            pltpu.VMEM(pair.shape, BF16),
            pltpu.VMEM(pair.shape, BF16),
            pltpu.VMEM(proj_weights.shape, BF16),
            pltpu.VMEM(out_weights.shape, BF16),
            pltpu.VMEM(norm_gains.shape, F32),
            pltpu.VMEM(norm_biases.shape, F32),
            pltpu.VMEM(block, BF16),
            pltpu.VMEM(block, BF16),
            pltpu.VMEM((tile, tile, 128), BF16),
            pltpu.VMEM((side * cells, 128), F32),
            pltpu.VMEM((side * cells, 128), F32),
            wide,
            wide,
            wide,
            wide,
            slim,
            wide,
            wide,
            wide,
            wide,
            wide,
            wide,
            slim,
            wide,
            wide,
            wide,
            wide,
            wide,
            pltpu.VMEM(block, BF16),
            pltpu.VMEM(block, BF16),
            pltpu.VMEM(block, BF16),
            pltpu.VMEM(block, BF16),
            pltpu.VMEM((3, 256, 128), BF16),
            pltpu.VMEM((3, side, rows, 128), BF16),
            pltpu.VMEM((3, rows, 128), BF16),
            pltpu.VMEM((3, side, rows, 128), BF16),
            pltpu.VMEM((3, side, rows, 128), BF16),
            pltpu.VMEM((8, 128), F32),
            pltpu.VMEM((1, side, 8, 128), F32),
            pltpu.VMEM((8, 128), F32),
            pltpu.VMEM((1, side, 8, 128), F32),
            dma((7,)),
            dma((side,)),
            dma((side,)),
            dma((side,)),
            dma((side,)),
            dma((2,)),
            dma((side,)),
            dma((side,)),
            dma((side,)),
            dma((side,)),
        ]
        + [dma((3 * side,))] * 6
        + [dma((side,))] * 4,
        compiler_params=pltpu.CompilerParams(
            collective_id=0, has_side_effects=True, vmem_limit_bytes=63 * 1024 * 1024
        ),
    )(token_mask, pair, cotangent, proj_weights, out_weights, norm_gains, norm_biases)
    main = pl.BlockSpec(memory_space=pltpu.HBM)
    return pl.pallas_call(
        hand_over,
        out_shape=tuple(jax.ShapeDtypeStruct(x.shape, x.dtype) for x in results),
        in_specs=[vmem] * 4,
        out_specs=(main,) * 4,
        scratch_shapes=[dma((4,))],
    )(*results)


def device_program(*args):
    rows, cols = lax.axis_size("row"), lax.axis_size("col")
    pair = args[0]
    square = rows == cols and pair.shape[0] == pair.shape[1] == 16
    if square and 256 % (16 * rows) == 0 and pair.shape[2] == 128:
        return fused(rows, *args)
    return per_device(*args)


def solution(mesh):
    in_specs = (
        P(("grp", "row"), "col", None),
        P(("grp", "row"), "col", None),
        P("grp"),
        P(),
        P(),
        P(),
        P(),
    )
    out_specs = (
        P(("grp", "row"), "col", None),
        P(("grp", "row"), "col", None),
        P("grp", None, None),
        P("grp", None),
    )
    return jax.shard_map(
        device_program, mesh=mesh, in_specs=in_specs, out_specs=out_specs, check_vma=False
    )
```
